256 devices in a mesh: row: 16 (over z, core), col: 4 (over x), ch: 4 (over y).
Axes of the slice: x: 4, y: 4, z: 8, core: 2. Of those that a mesh axis runs over, the one named last changes fastest.
Arguments:
- grad_out: float32 [32768, 1024], P(('row', 'col'), 'ch'), may hold values from -6 to 6
- relu_mask: int32 [32768, 1024], P(('row', 'col'), 'ch'), may hold values 0 or 1
- saved_agg: float32 [32768, 1024], P(('row', 'col'), 'ch'), may hold values from -0.1875 to 0.1875
- weight: float32 [1024, 1024], P('ch'), may hold values from -0.1875 to 0.1875
- tile_vals: float32 [16, 4, 128, 128, 128], P('row', 'col'), may hold values from -0.046875 to 0.046875
- tile_pos: int32 [16, 4, 128], P('row', 'col'), may hold values from 0 to 127, as said below
- tile_count: int32 [16, 4], P('row', 'col'), may hold values from 32 to 128, as said below
Outputs:
- weight_grad: float32 [1024, 1024], P(('row', 'col'), 'ch')
- input_grad: float32 [4096, 1024], P('col', 'ch')
The draws below stay inside these ranges and needn't reach their ends.
Inputs may be any that keep to these rules, and one draw needn't show every extreme that they name: `tile_pos`: each block's entries are a permutation of 0 to 127; the first tile_count of them are the block's nonzero tiles, the others list its zero tiles and their slots' values are ignored. `tile_count`: some block is full in every draw.
All inputs are finite; a program needn't handle non-finite values. No bound on the sum of `relu_mask` on one device may be relied on, other than what follows from the above.
Results may differ from the reference program's by a relative error of at most 0.0003.
Values sent between devices are 32-bit elements; how exact they have to be, the bound alone decides.
No kernel may reach another device: no remote copies, remote signals or barrier semaphores. Data moves between devices by JAX's collectives and lax.ppermute only.
A program may use at most 128 MiB of HBM per device.

```python
import jax
import jax.numpy as jnp
from jax import lax

F = 1024
TILE = 128
OUT_TILES = 16
IN_TILES = 8
BLOCK_TILES = 128
ROWS_OUT = 32768
ROWS_IN = 4096
N_ROW = 16
N_COL = 4


def draw_tile_pos(key, part):
    row_groups = ROWS_OUT // (TILE * OUT_TILES)
    col_groups = ROWS_IN // (TILE * IN_TILES)
    block_keys = jax.random.split(jax.random.fold_in(key, 11), row_groups * col_groups)
    orders = jax.vmap(lambda single: jax.random.permutation(single, BLOCK_TILES))(block_keys)
    return orders.reshape(row_groups, col_groups, BLOCK_TILES).astype(jnp.int32)


def draw_tile_count(key, part):
    row_groups = ROWS_OUT // (TILE * OUT_TILES)
    col_groups = ROWS_IN // (TILE * IN_TILES)
    lowest = max(BLOCK_TILES // 4, 1)
    counts = jax.random.randint(jax.random.fold_in(key, 23), (row_groups * col_groups,), lowest, BLOCK_TILES + 1)
    chosen = jax.random.randint(jax.random.fold_in(key, 29), (), 0, row_groups * col_groups)
    counts = jnp.where(jnp.arange(row_groups * col_groups, dtype=jnp.int32) == chosen, BLOCK_TILES, counts)
    return counts.reshape(row_groups, col_groups).astype(jnp.int32)


def touch_ends(array, stream_key, least, top_value):
    spot = [jax.random.randint(jax.random.fold_in(stream_key, axis), (), 0, length) for axis, length in enumerate(array.shape)]
    main_axis = array.shape.index(max(array.shape))
    next_to = spot[:main_axis] + [(spot[main_axis] + 1) % array.shape[main_axis]] + spot[main_axis + 1:]
    return array.at[tuple(spot)].set(least).at[tuple(next_to)].set(top_value)


def strengthened(drawn, key, source, target, blocks, factor):
    def block_of(dim):
        return (jnp.arange(drawn.shape[dim]) // (drawn.shape[dim] // blocks)).reshape((-1,) + (1,) * (drawn.ndim - 1 - dim))

    one_side = jax.random.permutation(key, blocks)[block_of(target)]
    other_side = (block_of(target) + blocks // 2) % blocks
    return jnp.where((block_of(source) == one_side) | (block_of(source) == other_side), factor * drawn, drawn)


def block_scale(rng, extent, cuts, least, largest):
    def one(axis_at, parts):
        draws = jax.random.uniform(jax.random.fold_in(jax.random.fold_in(rng, 6), axis_at), (parts,), jnp.float32, least / len(cuts), largest / len(cuts))
        return jnp.repeat(jnp.exp(draws), extent[axis_at] // parts).reshape((-1,) + (1,) * (len(extent) - axis_at - 1))

    factor_of = one(*cuts[0])
    for cut in cuts[1:]:
        factor_of = factor_of * one(*cut)
    return factor_of


def noise(own_key, shape, spread, limit, shards=(), held_as=jnp.bfloat16):
    factor_of = block_scale(own_key, shape, shards, -0.22, 0.18) if shards else 1.0
    drawn = jax.random.normal(own_key, shape, jnp.float32) * spread * factor_of
    return jnp.minimum(jnp.maximum(drawn, -limit), limit).astype(held_as)


def noise_with(rng, shape, width, bound, cuts, heavy, kind=jnp.bfloat16):
    result = width * jax.random.normal(rng, shape, jnp.float32)
    if cuts:
        result = result * block_scale(rng, shape, cuts, -0.22, 0.18)
    return jnp.clip(strengthened(result, jax.random.fold_in(rng, 3), *heavy), -bound, bound).astype(kind)


def setup_inputs(seed: int = 0) -> dict:
    splits = jax.random.split(jax.random.key(seed), 8)
    grad_out = noise(splits[0], (ROWS_OUT, F), 1.0, 6.0, ((0, 64), (1, 4)), jnp.float32)
    relu_mask = touch_ends((jax.random.randint(splits[1], (ROWS_OUT, F), 0, 2) < 1).astype(jnp.int32), jax.random.fold_in(splits[1], 1), 0, 1)
    saved_agg = noise_with(splits[2], (ROWS_OUT, F), (2.0 / ROWS_OUT ** 0.5), 0.1875, ((0, 64), (1, 4)), (0, 1, 64, 4.0), jnp.float32)
    weight = noise(splits[3], (F, F), F ** -0.5, 0.1875, ((0, 4),), jnp.float32)
    tile_vals = noise(splits[4], (N_ROW, N_COL, BLOCK_TILES, TILE, TILE), (TILE * OUT_TILES * N_ROW // 2) ** -0.5, 0.046875, ((0, 16), (1, 4)), jnp.float32)
    tile_pos = draw_tile_pos(jax.random.fold_in(splits[7], 71), 0)
    tile_count = draw_tile_count(jax.random.fold_in(splits[7], 71), 0)
    return dict(grad_out=grad_out, relu_mask=relu_mask, saved_agg=saved_agg, weight=weight, tile_vals=tile_vals, tile_pos=tile_pos, tile_count=tile_count)


HIGHEST = lax.Precision.HIGHEST

def block_grad(tile_set, positions, live_count, grad_rows):
    slot_total = tile_set.shape[0]
    channels = grad_rows.shape[1]
    active = (jnp.arange(slot_total, dtype=jnp.int32) < live_count).astype(jnp.float32)
    out_tile = (positions // IN_TILES).astype(jnp.int32)
    in_tile = (positions % IN_TILES).astype(jnp.int32)
    blocks = grad_rows.reshape(OUT_TILES, TILE, channels)
    picked = jnp.take(blocks, out_tile, axis=0)
    product = jnp.einsum('tij,tif->tjf', tile_set, picked, precision=HIGHEST)
    onehot = (in_tile[:, None] == jnp.arange(IN_TILES, dtype=jnp.int32)[None, :]).astype(jnp.float32) * active[:, None]
    summed = jnp.einsum('tc,tjf->cjf', onehot, product, precision=HIGHEST)
    return summed.reshape(IN_TILES * TILE, channels)

def reference(grad_out, relu_mask, saved_agg, weight, tile_vals, tile_pos, tile_count):
    masked = grad_out * relu_mask.astype(jnp.float32)
    weight_grad = jnp.dot(saved_agg.T, masked, precision=HIGHEST, preferred_element_type=jnp.float32)
    agg_grad = jnp.dot(masked, weight.T, precision=HIGHEST, preferred_element_type=jnp.float32)
    row_groups = tile_vals.shape[0]
    col_groups = tile_vals.shape[1]
    channels = agg_grad.shape[1]
    grad_blocks = agg_grad.reshape(row_groups, OUT_TILES * TILE, channels)

    def per_column(col_index):

        def add_block(running, row_index):
            return (running + block_grad(tile_vals[row_index, col_index], tile_pos[row_index, col_index], tile_count[row_index, col_index], grad_blocks[row_index]), None)
        running, _ = lax.scan(add_block, jnp.zeros((IN_TILES * TILE, channels), jnp.float32), jnp.arange(row_groups, dtype=jnp.int32))
        return running
    input_grad = lax.map(per_column, jnp.arange(col_groups, dtype=jnp.int32))
    return (weight_grad, input_grad.reshape(col_groups * IN_TILES * TILE, channels))
```

```python
import functools

import jax
import jax.numpy as jnp
from jax import lax
from jax.experimental import pallas as pl
from jax.experimental.pallas import tpu as pltpu
from jax.sharding import PartitionSpec as P

F32 = jnp.float32
BF16 = jnp.bfloat16
MB = 1 << 20
GROUP = 16
NN = (((1,), (0,)), ((), ()))
TN = (((0,), (0,)), ((), ()))
NT = (((1,), (1,)), ((), ()))

AGG_PAIRS = [(0, 1), (1, 0), (2, 3), (3, 2)]
MASK_PAIRS = [(0, 3), (3, 0), (1, 2), (2, 1)]
CORE = [(r, r ^ 1) for r in range(16)]


def z_shift(d):
    return [(r, ((r // 2 + d) % 8) * 2 + r % 2) for r in range(16)]


def ring4(d):
    return [(i, (i + d) % 4) for i in range(4)]


def last_swap():
    pairs = []
    mate = dict(MASK_PAIRS)
    for r in range(16):
        for k in range(4):
            if (r >= 8) == (k < 2):
                pairs.append((r * 4 + k, (r ^ 8) * 4 + mate[k]))
    return pairs


def params(mb=32):
    return pltpu.CompilerParams(vmem_limit_bytes=mb * MB)


def shape(*dims, dtype=F32):
    return jax.ShapeDtypeStruct(dims, dtype)


def split(x):
    hi = x.astype(BF16)
    return hi, (x - hi.astype(F32)).astype(BF16)


def dot3(a, b, dims):
    (ah, al), (bh, bl) = a, b

    def one(p, q):
        return lax.dot_general(p, q, dims, preferred_element_type=F32)

    return one(ah, bh) + (one(ah, bl) + one(al, bh))


def mask_kernel(g_ref, m_ref, a_ref, b_ref, full_ref):
    masked = g_ref[...] * m_ref[...].astype(F32)
    full_ref[...] = masked
    a_ref[...] = masked[:256]
    b_ref[...] = masked[256:]


def prep_kernel(pos_ref, cnt_ref, tv_ref, hi_ref, lo_ref):
    g = pl.program_id(0)
    cnt = cnt_ref[0]

    def body(i, carry):
        s = g * GROUP + i
        p = pos_ref[s]
        out_tile = p // 8
        hi, lo = split(jnp.where(s < cnt, tv_ref[i], 0.0).T)
        rows = pl.ds(pl.multiple_of((p % 8) * 128, 128), 128)
        cols = pl.ds(pl.multiple_of((out_tile % 2) * 128, 128), 128)
        hi_ref[out_tile // 2, rows, cols] = hi
        lo_ref[out_tile // 2, rows, cols] = lo
        return carry

    lax.fori_loop(0, GROUP, body, 0, unroll=4)


def prep(tile_vals, pos, cnt):
    return pl.pallas_call(
        prep_kernel,
        grid_spec=pltpu.PrefetchScalarGridSpec(
            num_scalar_prefetch=2,
            grid=(128 // GROUP,),
            in_specs=[pl.BlockSpec((GROUP, 128, 128), lambda g, *_: (g, 0, 0))],
            out_specs=[pl.BlockSpec((8, 1024, 256), lambda g, *_: (0, 0, 0))] * 2,
        ),
        out_shape=[shape(8, 1024, 256, dtype=BF16)] * 2,
        compiler_params=params(40),
        name="prep",
    )(pos, cnt, tile_vals)


def pieces_kernel(n, has_base, is_last, at_ref, *refs):
    his, los, ms = refs[:n], refs[n : 2 * n], refs[2 * n : 3 * n]
    rest = refs[3 * n :]
    acc = None
    for j in range(n):
        term = dot3((his[j][0], los[j][0]), split(ms[j][...]), NN)
        acc = term if acc is None else acc + term
    if has_base:
        acc = acc + rest[0][...]
        rest = rest[1:]
    if is_last:
        i = pl.program_id(0)

        @pl.when(i == 0)
        def _():
            rest[0][...] = acc

        @pl.when(i == 1)
        def _():
            rest[1][...] = acc
    else:
        rest[0][...] = acc


def pieces(at, hi, lo, ms, places, base=None, last=False):
    n = len(ms)

    def half(i, at):
        core = at[0] % 2
        return i + (1 - 2 * i) * (1 - core) if last else i

    def a_map(place, i, at):
        off, part = place
        return (2 * ((at[1] + off) % 4) + part, half(i, at), 0)

    a_specs = [pl.BlockSpec((1, 512, 256), functools.partial(a_map, p)) for p in places]
    specs = a_specs + a_specs + [pl.BlockSpec((256, 256), lambda i, at: (0, 0))] * n
    args = [hi] * n + [lo] * n + list(ms)
    if base is not None:
        specs.append(pl.BlockSpec((512, 256), lambda i, at: (half(i, at), 0)))
        args.append(base)
    if last:
        out_specs = [pl.BlockSpec((512, 256), lambda i, at: (0, 0))] * 2
        out_shape = [shape(512, 256)] * 2
    else:
        out_specs = pl.BlockSpec((512, 256), lambda i, at: (i, 0))
        out_shape = shape(1024, 256)
    return pl.pallas_call(
        functools.partial(pieces_kernel, n, base is not None, last),
        grid_spec=pltpu.PrefetchScalarGridSpec(
            num_scalar_prefetch=1, grid=(2,), in_specs=specs, out_specs=out_specs
        ),
        out_shape=out_shape,
        compiler_params=params(),
        name="pieces_last" if last else "pieces",
    )(at, *args)


def wgrad_kernel(at_ref, a0, a1, m0, m1, keep, send, res):
    row, k = at_ref[0], at_ref[2]
    core = row % 2
    aggs = [split(a0[...]), split(a1[...])]
    grads = [split(m0[...]), split(m1[...])]
    own_part = k // 2
    for i in range(2):
        rows = pl.ds(pl.multiple_of(((k + i) % 2) * 256, 256), 256)
        res[own_part, rows, :] = dot3(aggs[i], grads[0], TN)
        res[1 - own_part, rows, :] = dot3(aggs[i], grads[1], TN)
    for part in range(2):
        for zz in range(4):
            for c in range(4):
                to = slice((part * 4 + zz) * 16, (part * 4 + zz) * 16 + 16)
                mine = pl.multiple_of(zz * 128 + core * 64 + c * 16, 16)
                other = pl.multiple_of(zz * 128 + (1 - core) * 64 + c * 16, 16)
                keep[c, to, :] = res[part, pl.ds(mine, 16), :]
                send[c, to, :] = res[part, pl.ds(other, 16), :]


def spread_kernel(n, axis, at_ref, keep, recv, *outs):
    me = at_ref[1] if axis == "col" else at_ref[0] // 2
    for d in range(n):
        j = (me + d) % n
        outs[d][...] = keep[j] + recv[j]


def finish_kernel(at_ref, h0, h1, h2, h3, w_ref, t0, t1, t2, t3, own_out, own_w, *msgs):
    z, k = at_ref[0] // 2, at_ref[2]
    acc = None
    for d, h in enumerate((h0, h1, h2, h3)):
        co = pl.multiple_of(((k + 4 - d) % 4) * 256, 256)
        term = dot3(split(h[...]), split(w_ref[:, pl.ds(co, 256)]), NT)
        acc = term if acc is None else acc + term
    own_out[...] = acc

    def share(j):
        rows = pl.ds(pl.multiple_of(j * 16, 16), 16)
        return (t0[rows, :] + t1[rows, :]) + (t2[rows, :] + t3[rows, :])

    own_w[...] = share(z)
    for d in range(1, 8):
        msgs[d - 1][:64, :] = acc
        msgs[d - 1][64:, :] = share((z + d) % 8)


def gather_kernel(at_ref, own_out, own_w, *refs):
    z = at_ref[0] // 2
    msgs, half, w = refs[:7], refs[7], refs[8]
    half[z] = own_out[...]
    total = own_w[...]
    for d in range(1, 8):
        half[(z + 8 - d) % 8] = msgs[d - 1][:64, :]
        total += msgs[d - 1][64:, :]
    w[...] = total


def last_kernel(at_ref, half, other, w, w_recv, out, w_out):
    row, k = at_ref[0], at_ref[2]
    core = row % 2
    out[core] = half[...]
    out[1 - core] = other[...]
    keeps = (row // 8) == (k // 2)
    w_out[...] = jnp.where(keeps, w[...], w_recv[...])


def call(kernel, name, out_shape, at, *args, scratch=()):
    return pl.pallas_call(
        kernel,
        grid_spec=pltpu.PrefetchScalarGridSpec(
            num_scalar_prefetch=1,
            grid=(1,),
            in_specs=[pl.BlockSpec(a.shape, functools.partial(lambda n, i, at: (0,) * n, a.ndim)) for a in args],
            out_specs=[
                pl.BlockSpec(s.shape, functools.partial(lambda n, i, at: (0,) * n, len(s.shape)))
                for s in out_shape
            ],
            scratch_shapes=list(scratch),
        ),
        out_shape=out_shape,
        compiler_params=params(),
        name=name,
    )(at, *args)


def per_device(grad_out, relu_mask, saved_agg, weight, tile_vals, tile_pos, tile_count):
    pp = lax.ppermute
    at = jnp.stack([lax.axis_index("row"), lax.axis_index("col"), lax.axis_index("ch")]).astype(jnp.int32)
    a, b, masked = pl.pallas_call(
        mask_kernel,
        out_shape=[shape(256, 256), shape(256, 256), shape(512, 256)],
        compiler_params=params(),
        name="mask",
    )(grad_out, relu_mask)
    la, rb = pp(a, "col", ring4(1)), pp(b, "col", ring4(-1))
    lb, ra = pp(b, "col", ring4(1)), pp(a, "col", ring4(-1))
    oa, ob = pp(la, "col", ring4(1)), pp(rb, "col", ring4(-1))
    agg_mate = pp(saved_agg, "ch", AGG_PAIRS)
    masked_mate = pp(masked, "ch", MASK_PAIRS)

    hi, lo = prep(tile_vals.reshape(128, 128, 128), tile_pos.reshape(128), tile_count.reshape(1))
    part = pieces(at, hi, lo, [a, b, la, rb], [(0, 0), (0, 1), (3, 0), (1, 1)])
    part = pieces(at, hi, lo, [lb, ra], [(3, 1), (1, 0)], base=part)
    send, keep = pieces(at, hi, lo, [oa, ob], [(2, 0), (2, 1)], base=part, last=True)

    w_keep, w_send = call(
        wgrad_kernel, "wgrad", [shape(4, 128, 256)] * 2, at, saved_agg, agg_mate, masked, masked_mate,
        scratch=[pltpu.VMEM((2, 512, 256), F32)],
    )
    w_recv = pp(w_send, "row", CORE)
    w_parts = call(
        functools.partial(spread_kernel, 4, "col"), "w_spread", [shape(128, 256)] * 4, at, w_keep, w_recv
    )
    t = [w_parts[0]] + [pp(w_parts[d], "col", ring4(d)) for d in (1, 2, 3)]

    recv = pp(send, "row", CORE)
    h_parts = call(
        functools.partial(spread_kernel, 8, "z"), "h_spread", [shape(64, 256)] * 8, at,
        keep.reshape(8, 64, 256), recv.reshape(8, 64, 256),
    )
    h = h_parts[0]
    for d in range(1, 8):
        h = h + pp(h_parts[d], "row", z_shift(d))
    hs = [h] + [pp(h, "ch", ring4(d)) for d in (1, 2, 3)]
    own_out, own_w, *msgs = call(
        finish_kernel, "finish", [shape(64, 256), shape(16, 256)] + [shape(80, 256)] * 7, at, *hs, weight, *t
    )
    got = [pp(msgs[d - 1], "row", z_shift(d)) for d in range(1, 8)]
    half, w_sum = call(
        gather_kernel, "gather", [shape(8, 64, 256), shape(16, 256)], at, own_out, own_w, *got
    )
    half = half.reshape(512, 256)
    other = pp(half, "row", CORE)
    w_other = pp(w_sum, ("row", "ch"), last_swap())
    input_grad, weight_grad = call(
        last_kernel, "last", [shape(2, 512, 256), shape(16, 256)], at, half, other, w_sum, w_other
    )
    return weight_grad, input_grad.reshape(1024, 256)


def solution(mesh):
    in_specs = (
        P(("row", "col"), "ch"),
        P(("row", "col"), "ch"),
        P(("row", "col"), "ch"),
        P("ch", None),
        P("row", "col", None, None, None),
        P("row", "col", None),
        P("row", "col"),
    )
    out_specs = (P(("row", "col"), "ch"), P("col", "ch"))
    return jax.shard_map(
        per_device, mesh=mesh, in_specs=in_specs, out_specs=out_specs, check_vma=False
    )
```

```python
import functools

import jax
import jax.numpy as jnp
from jax import lax
from jax.experimental import pallas as pl
from jax.experimental.pallas import tpu as pltpu
from jax.sharding import PartitionSpec as P

F32 = jnp.float32
BF16 = jnp.bfloat16
MB = 1 << 20
GROUP = 16
NN = (((1,), (0,)), ((), ()))
TN = (((0,), (0,)), ((), ()))
NT = (((1,), (1,)), ((), ()))

AGG_PAIRS = [(0, 1), (1, 0), (2, 3), (3, 2)]
MASK_PAIRS = [(0, 3), (3, 0), (1, 2), (2, 1)]
CORE = [(r, r ^ 1) for r in range(16)]


FAR_FIRST = (4, 3, 5, 2, 6, 1, 7)


def z_shift(d):
    return [(r, ((r // 2 + d) % 8) * 2 + r % 2) for r in range(16)]


def ring4(d):
    return [(i, (i + d) % 4) for i in range(4)]


def params(mb=32):
    return pltpu.CompilerParams(vmem_limit_bytes=mb * MB)


def shape(*dims, dtype=F32):
    return jax.ShapeDtypeStruct(dims, dtype)


def split(x):
    hi = x.astype(BF16)
    return hi, (x - hi.astype(F32)).astype(BF16)


def dot3(a, b, dims):
    (ah, al), (bh, bl) = a, b

    def one(p, q):
        return lax.dot_general(p, q, dims, preferred_element_type=F32)

    return one(ah, bh) + (one(ah, bl) + one(al, bh))


VMEM = pl.BlockSpec(memory_space=pltpu.VMEM)
SMEM = pl.BlockSpec(memory_space=pltpu.SMEM)
HBM = pl.BlockSpec(memory_space=pltpu.HBM)


def call(kernel, name, out_shape, *args, scalars=1, in_hbm=(), out_hbm=(), scratch=(), mb=12, alias=None):
    ins = [SMEM] * scalars + [HBM if i in in_hbm else VMEM for i in range(len(args) - scalars)]
    outs = [HBM if i in out_hbm else VMEM for i in range(len(out_shape))]
    return pl.pallas_call(
        kernel,
        in_specs=ins,
        out_specs=outs,
        out_shape=out_shape,
        scratch_shapes=list(scratch),
        input_output_aliases=alias or {},
        compiler_params=params(mb),
        name=name,
    )(*args)


def mask_kernel(g_ref, m_ref, full_ref):
    full_ref[...] = g_ref[...] * m_ref[...].astype(F32)


def halves_kernel(left_ref, right_ref, after_ref, a_ref, b_ref):
    a_ref[...] = left_ref[:256, :]
    b_ref[...] = right_ref[256:, :]


def prep_kernel(pos_ref, cnt_ref, tv_hbm, hi_ref, lo_ref, tv_ref, sems):
    cnt = cnt_ref[0]
    chunks = 128 // GROUP
    copies = []
    for g in range(chunks):
        slots = pl.ds(g * GROUP, GROUP)
        copies.append(pltpu.make_async_copy(tv_hbm.at[slots], tv_ref.at[slots], sems.at[g]))
    for copy in copies:
        copy.start()

    def body(s, carry):
        p = pos_ref[s]
        out_tile = p // 8
        hi, lo = split(jnp.where(s < cnt, tv_ref[s], 0.0).T)
        rows = pl.ds(pl.multiple_of((p % 8) * 128, 128), 128)
        cols = pl.ds(pl.multiple_of((out_tile % 2) * 128, 128), 128)
        hi_ref[out_tile // 2, rows, cols] = hi
        lo_ref[out_tile // 2, rows, cols] = lo
        return carry

    for g in range(chunks):
        copies[g].wait()
        lax.fori_loop(g * GROUP, (g + 1) * GROUP, body, 0, unroll=8)


def prep(pos, cnt, tile_vals):
    return call(
        prep_kernel, "prep", [shape(8, 1024, 256, dtype=BF16)] * 2, pos, cnt, tile_vals,
        scalars=2, in_hbm=(0,), mb=40,
        scratch=[pltpu.VMEM((128, 128, 128), F32), pltpu.SemaphoreType.DMA((128 // GROUP,))],
    )


def pieces_kernel(places, has_base, is_last, at_ref, hi_ref, lo_ref, *refs):
    n = len(places)
    core, col = at_ref[0] % 2, at_ref[1]
    ms, rest = refs[:n], refs[n:]
    base = rest[0] if has_base else None
    outs = rest[-2:] if is_last else rest[-1:]
    parts, index = [], []
    for m, (off, part) in zip(ms, places):
        rows = slice(256 * part, 256 * part + 256) if m.shape[0] == 512 else slice(0, 256)
        parts.append(split(m[rows, :]))
        index.append(2 * ((col + off) % 4) + part)
    for i in range(2):
        start = 512 * (i + (1 - 2 * i) * (1 - core)) if is_last else 512 * i
        rows = pl.ds(pl.multiple_of(start, 512), 512)
        acc = None
        for j in range(n):
            term = dot3((hi_ref[index[j], rows, :], lo_ref[index[j], rows, :]), parts[j], NN)
            acc = term if acc is None else acc + term
        if has_base:
            acc = acc + base[rows, :]
        if is_last:
            outs[i][...] = acc
        else:
            outs[0][rows, :] = acc


def pieces(at, hi, lo, ms, places, base=None, after=None, last=False):
    return call(
        functools.partial(pieces_kernel, places, base is not None, last),
        "pieces_last" if last else "pieces",
        [shape(512, 256)] * 2 if last else [shape(1024, 256)],
        at, hi, lo, *ms, *([] if base is None else [base]), *([] if after is None else [after]),
    )


def wgrad_kernel(at_ref, a0, a1, m0, m1, keep, send, token, res):
    core, k = at_ref[0] % 2, at_ref[2]
    token[...] = jnp.zeros_like(token)
    aggs = [split(a0[...]), split(a1[...])]
    grads = [split(m0[...]), split(m1[...])]
    for i in range(2):
        rows = pl.ds(pl.multiple_of(((k + i) % 2) * 256, 256), 256)
        for part in range(2):
            res[part, rows, :] = dot3(aggs[i], grads[part], TN)
    for part in range(2):
        for zz in range(4):
            for c in range(4):
                to = slice((part * 4 + zz) * 16, (part * 4 + zz) * 16 + 16)
                mine = pl.multiple_of(zz * 128 + core * 64 + c * 16, 16)
                other = pl.multiple_of(zz * 128 + (1 - core) * 64 + c * 16, 16)
                keep[c, to, :] = res[part, pl.ds(mine, 16), :]
                send[c, to, :] = res[part, pl.ds(other, 16), :]


def w_parts_kernel(keep, recv, own, other):
    for c in range(4):
        own[c] = keep[c, :64, :] + recv[c, :64, :]
        other[c] = keep[c, 64:, :] + recv[c, 64:, :]


def w_spread_kernel(at_ref, own, recv, after_ref, *outs):
    c, h = at_ref[1], at_ref[2] // 2
    mine = pl.ds(pl.multiple_of(h * 64, 64), 64)
    theirs = pl.ds(pl.multiple_of((1 - h) * 64, 64), 64)
    for d in range(4):
        j = (c + d) % 4
        outs[d][mine, :] = own[j]
        outs[d][theirs, :] = recv[j]


def spread_kernel(at_ref, keep, recv, *outs):
    z = at_ref[0] // 2
    for i, d in enumerate((0,) + FAR_FIRST):
        j = (z + d) % 8
        outs[i][...] = keep[j] + recv[j]


def total_kernel(after_ref, *refs):
    total = refs[0][...]
    for r in refs[1:-1]:
        total = total + r[...]
    refs[-1][...] = total


def finish_kernel(at_ref, h0, h1, h2, h3, w_ref, t0, t1, t2, t3, own_out, own_w, *msgs):
    z, k = at_ref[0] // 2, at_ref[2]
    acc = None
    for d, h in enumerate((h0, h1, h2, h3)):
        co = pl.multiple_of(((k + 4 - d) % 4) * 256, 256)
        term = dot3(split(h[...]), split(w_ref[:, pl.ds(co, 256)]), NT)
        acc = term if acc is None else acc + term
    own_out[...] = acc

    def share(j):
        rows = pl.ds(pl.multiple_of(j * 16, 16), 16)
        return (t0[rows, :] + t1[rows, :]) + (t2[rows, :] + t3[rows, :])

    own_w[...] = share(z)
    for msg, d in zip(msgs, FAR_FIRST):
        msg[:64, :] = acc
        msg[64:, :] = share((z + d) % 8)


def gather_kernel(at_ref, own_out, own_w, *refs):
    z = at_ref[0] // 2
    msgs, half, w = refs[:7], refs[7], refs[8]
    half[z] = own_out[...]
    total = own_w[...]
    for msg, d in zip(msgs, FAR_FIRST):
        half[(z + 8 - d) % 8] = msg[:64, :]
        total += msg[64:, :]
    w[...] = total


def last_kernel(at_ref, half, other, out, sems):
    core = at_ref[0] % 2
    copies = []
    for i in range(4):
        rows = pl.ds(i * 128, 128)
        copies.append(pltpu.make_async_copy(half.at[rows], out.at[core, rows], sems.at[0, i]))
        copies.append(pltpu.make_async_copy(other.at[rows], out.at[1 - core, rows], sems.at[1, i]))
    for copy in copies:
        copy.start()
    for copy in copies:
        copy.wait()


def per_device(grad_out, relu_mask, saved_agg, weight, tile_vals, tile_pos, tile_count):
    pp = lax.ppermute
    at = jnp.stack([lax.axis_index("row"), lax.axis_index("col"), lax.axis_index("ch")]).astype(jnp.int32)
    (masked,) = call(mask_kernel, "mask", [shape(512, 256)], grad_out, relu_mask, scalars=0)
    left, right = pp(masked, "col", ring4(1)), pp(masked, "col", ring4(-1))
    agg_mate = pp(saved_agg, "ch", AGG_PAIRS)
    masked_mate = pp(masked, "ch", MASK_PAIRS)

    hi, lo = prep(tile_pos.reshape(128), tile_count.reshape(1), tile_vals.reshape(128, 128, 128))
    (part,) = pieces(at, hi, lo, [masked, masked], [(0, 0), (0, 1)])
    la, rb = call(halves_kernel, "halves", [shape(256, 256)] * 2, left, right, part, scalars=0)
    oa, ob = pp(la, "col", ring4(1)), pp(rb, "col", ring4(-1))
    (part,) = pieces(at, hi, lo, [la, left, right, rb], [(3, 0), (3, 1), (1, 0), (1, 1)], base=part)
    w_keep, w_send, token = call(
        wgrad_kernel, "wgrad", [shape(4, 128, 256)] * 2 + [shape(8, 128)], at, saved_agg, agg_mate, masked, masked_mate,
        scratch=[pltpu.VMEM((2, 512, 256), F32)],
    )
    w_recv = pp(w_send, "row", CORE)
    send, keep = pieces(at, hi, lo, [oa, ob], [(2, 0), (2, 1)], base=part, after=token, last=True)

    recv = pp(send, "row", CORE)
    w_own, w_other = call(w_parts_kernel, "w_parts", [shape(4, 64, 256)] * 2, w_keep, w_recv, scalars=0)
    w_mate = pp(w_other, "ch", MASK_PAIRS)
    h_parts = call(
        spread_kernel, "h_spread", [shape(64, 256)] * 8, at, keep.reshape(8, 64, 256), recv.reshape(8, 64, 256)
    )
    h_got = [pp(p, "row", z_shift(d)) for p, d in zip(h_parts[1:], FAR_FIRST)]
    w_msgs = call(w_spread_kernel, "w_spread", [shape(128, 256)] * 4, at, w_own, w_mate, h_got[2])
    t = [w_msgs[0]] + [pp(w_msgs[d], "col", ring4(d)) for d in (1, 2, 3)]
    (h,) = call(total_kernel, "h_total", [shape(64, 256)], w_msgs[0], h_parts[0], *h_got, scalars=0)
    hs = [h] + [pp(h, "ch", ring4(d)) for d in (1, 2, 3)]
    own_out, own_w, *msgs = call(
        finish_kernel, "finish", [shape(64, 256), shape(16, 256)] + [shape(80, 256)] * 7, at, *hs, weight, *t
    )
    got = [pp(msg, "row", z_shift(d)) for msg, d in zip(msgs, FAR_FIRST)]
    half, weight_grad = call(
        gather_kernel, "gather", [shape(8, 64, 256), shape(16, 256)], at, own_out, own_w, *got
    )
    half = half.reshape(512, 256)
    other = pp(half, "row", CORE)
    (input_grad,) = call(
        last_kernel, "last", [shape(2, 512, 256)], at, half, other, out_hbm=(0,),
        scratch=[pltpu.SemaphoreType.DMA((2, 4))],
    )
    return weight_grad, input_grad.reshape(1024, 256)


def solution(mesh):
    in_specs = (
        P(("row", "col"), "ch"),
        P(("row", "col"), "ch"),
        P(("row", "col"), "ch"),
        P("ch", None),
        P("row", "col", None, None, None),
        P("row", "col", None),
        P("row", "col"),
    )
    out_specs = (P(("row", "col"), "ch"), P("col", "ch"))
    return jax.shard_map(
        per_device, mesh=mesh, in_specs=in_specs, out_specs=out_specs, check_vma=False
    )
```

```python
import functools

import jax
import jax.numpy as jnp
from jax import lax
from jax.experimental import pallas as pl
from jax.experimental.pallas import tpu as pltpu
from jax.sharding import PartitionSpec as P

F32 = jnp.float32
BF16 = jnp.bfloat16
MB = 1 << 20
GROUP = 16
NN = (((1,), (0,)), ((), ()))
TN = (((0,), (0,)), ((), ()))
NT = (((1,), (1,)), ((), ()))

AGG_PAIRS = [(0, 1), (1, 0), (2, 3), (3, 2)]
MASK_PAIRS = [(0, 3), (3, 0), (1, 2), (2, 1)]
CORE = [(r, r ^ 1) for r in range(16)]


PAIR = [(r, ((r // 2 + 1 - 2 * ((r // 2 + r) % 2)) % 8) * 2 + r % 2) for r in range(16)]
FAR_FIRST = (4, 3, 5, 2, 6, 1, 7)


def z_shift(d):
    return [(r, ((r // 2 + d) % 8) * 2 + r % 2) for r in range(16)]


def ring4(d):
    return [(i, (i + d) % 4) for i in range(4)]


def params(mb=32):
    return pltpu.CompilerParams(vmem_limit_bytes=mb * MB)


def shape(*dims, dtype=F32):
    return jax.ShapeDtypeStruct(dims, dtype)


def split(x):
    hi = x.astype(BF16)
    return hi, (x - hi.astype(F32)).astype(BF16)


def dot3(a, b, dims):
    (ah, al), (bh, bl) = a, b

    def one(p, q):
        return lax.dot_general(p, q, dims, preferred_element_type=F32)

    return one(ah, bh) + (one(ah, bl) + one(al, bh))


VMEM = pl.BlockSpec(memory_space=pltpu.VMEM)
SMEM = pl.BlockSpec(memory_space=pltpu.SMEM)
HBM = pl.BlockSpec(memory_space=pltpu.HBM)


def call(kernel, name, out_shape, *args, scalars=1, in_hbm=(), out_hbm=(), scratch=(), mb=12, alias=None):
    ins = [SMEM] * scalars + [HBM if i in in_hbm else VMEM for i in range(len(args) - scalars)]
    outs = [HBM if i in out_hbm else VMEM for i in range(len(out_shape))]
    return pl.pallas_call(
        kernel,
        in_specs=ins,
        out_specs=outs,
        out_shape=out_shape,
        scratch_shapes=list(scratch),
        input_output_aliases=alias or {},
        compiler_params=params(mb),
        name=name,
    )(*args)


def mask_kernel(g_ref, m_ref, full_ref):
    full_ref[...] = g_ref[...] * m_ref[...].astype(F32)


def halves_kernel(left_ref, right_ref, after_ref, a_ref, b_ref):
    a_ref[...] = left_ref[:256, :]
    b_ref[...] = right_ref[256:, :]


def prep_kernel(pos_ref, cnt_ref, tv_hbm, hi_ref, lo_ref, tv_ref, sems):
    cnt = cnt_ref[0]
    chunks = 128 // GROUP
    copies = []
    for g in range(chunks):
        slots = pl.ds(g * GROUP, GROUP)
        copies.append(pltpu.make_async_copy(tv_hbm.at[slots], tv_ref.at[slots], sems.at[g]))
    for copy in copies:
        copy.start()

    def body(s, carry):
        p = pos_ref[s]
        out_tile = p // 8
        hi, lo = split(jnp.where(s < cnt, tv_ref[s], 0.0).T)
        rows = pl.ds(pl.multiple_of((p % 8) * 128, 128), 128)
        cols = pl.ds(pl.multiple_of((out_tile % 2) * 128, 128), 128)
        hi_ref[out_tile // 2, rows, cols] = hi
        lo_ref[out_tile // 2, rows, cols] = lo
        return carry

    for g in range(chunks):
        copies[g].wait()
        lax.fori_loop(g * GROUP, (g + 1) * GROUP, body, 0, unroll=8)


def prep(pos, cnt, tile_vals):
    return call(
        prep_kernel, "prep", [shape(8, 1024, 256, dtype=BF16)] * 2, pos, cnt, tile_vals,
        scalars=2, in_hbm=(0,), mb=40,
        scratch=[pltpu.VMEM((128, 128, 128), F32), pltpu.SemaphoreType.DMA((128 // GROUP,))],
    )


def pieces_kernel(places, has_base, is_last, at_ref, hi_ref, lo_ref, *refs):
    n = len(places)
    core, col = at_ref[0] % 2, at_ref[1]
    ms, rest = refs[:n], refs[n:]
    base = rest[0] if has_base else None
    outs = rest[-2:] if is_last else rest[-1:]
    parts, index = [], []
    for m, (off, part) in zip(ms, places):
        rows = slice(256 * part, 256 * part + 256) if m.shape[0] == 512 else slice(0, 256)
        parts.append(split(m[rows, :]))
        index.append(2 * ((col + off) % 4) + part)
    for i in range(2):
        start = 512 * (i + (1 - 2 * i) * (1 - core)) if is_last else 512 * i
        rows = pl.ds(pl.multiple_of(start, 512), 512)
        acc = None
        for j in range(n):
            term = dot3((hi_ref[index[j], rows, :], lo_ref[index[j], rows, :]), parts[j], NN)
            acc = term if acc is None else acc + term
        if has_base:
            acc = acc + base[rows, :]
        if is_last:
            outs[i][...] = acc
        else:
            outs[0][rows, :] = acc


def pieces(at, hi, lo, ms, places, base=None, after=None, last=False):
    return call(
        functools.partial(pieces_kernel, places, base is not None, last),
        "pieces_last" if last else "pieces",
        [shape(512, 256)] * 2 if last else [shape(1024, 256)],
        at, hi, lo, *ms, *([] if base is None else [base]), *([] if after is None else [after]),
    )


def wgrad_kernel(at_ref, a0, a1, m0, m1, keep, send, token, res):
    core, k = at_ref[0] % 2, at_ref[2]
    token[...] = jnp.zeros_like(token)
    aggs = [split(a0[...]), split(a1[...])]
    grads = [split(m0[...]), split(m1[...])]
    for i in range(2):
        rows = pl.ds(pl.multiple_of(((k + i) % 2) * 256, 256), 256)
        for part in range(2):
            res[part, rows, :] = dot3(aggs[i], grads[part], TN)
    for part in range(2):
        for zz in range(4):
            for c in range(4):
                to = slice((part * 4 + zz) * 16, (part * 4 + zz) * 16 + 16)
                mine = pl.multiple_of(zz * 128 + core * 64 + c * 16, 16)
                other = pl.multiple_of(zz * 128 + (1 - core) * 64 + c * 16, 16)
                keep[c, to, :] = res[part, pl.ds(mine, 16), :]
                send[c, to, :] = res[part, pl.ds(other, 16), :]


def w_parts_kernel(keep, recv, own, other):
    for c in range(4):
        own[c] = keep[c, :64, :] + recv[c, :64, :]
        other[c] = keep[c, 64:, :] + recv[c, 64:, :]


def w_spread_kernel(at_ref, own, recv, after_ref, *outs):
    c, h = at_ref[1], at_ref[2] // 2
    mine = pl.ds(pl.multiple_of(h * 64, 64), 64)
    theirs = pl.ds(pl.multiple_of((1 - h) * 64, 64), 64)
    for d in range(4):
        j = (c + d) % 4
        outs[d][mine, :] = own[j]
        outs[d][theirs, :] = recv[j]


def h_first_kernel(at_ref, keep, recv, kept, send):
    core, z = at_ref[0] % 2, at_ref[0] // 2
    mate = z + 1 - 2 * ((z + core) % 2)
    for j in range(4):
        a, b = (z + 2 * j) % 8, (mate + 8 + 2 * j) % 8
        kept[j] = keep[a] + recv[a]
        send[j] = keep[b] + recv[b]


def h_second_kernel(after_ref, kept, recv, *outs):
    for j in range(4):
        outs[j][...] = kept[j] + recv[j]


def total_kernel(*refs):
    total = refs[0][...]
    for r in refs[1:-1]:
        total = total + r[...]
    refs[-1][...] = total


def finish_kernel(at_ref, h0, h1, h2, h3, w_ref, t0, t1, t2, t3, own_out, own_w, *msgs):
    z, k = at_ref[0] // 2, at_ref[2]
    acc = None
    for d, h in enumerate((h0, h1, h2, h3)):
        co = pl.multiple_of(((k + 4 - d) % 4) * 256, 256)
        term = dot3(split(h[...]), split(w_ref[:, pl.ds(co, 256)]), NT)
        acc = term if acc is None else acc + term
    own_out[...] = acc

    def share(j):
        rows = pl.ds(pl.multiple_of(j * 16, 16), 16)
        return (t0[rows, :] + t1[rows, :]) + (t2[rows, :] + t3[rows, :])

    own_w[...] = share(z)
    for msg, d in zip(msgs, FAR_FIRST):
        msg[:64, :] = acc
        msg[64:, :] = share((z + d) % 8)


def gather_kernel(at_ref, own_out, own_w, *refs):
    z = at_ref[0] // 2
    msgs, half, w = refs[:7], refs[7], refs[8]
    half[z] = own_out[...]
    total = own_w[...]
    for msg, d in zip(msgs, FAR_FIRST):
        half[(z + 8 - d) % 8] = msg[:64, :]
        total += msg[64:, :]
    w[...] = total


def last_kernel(at_ref, half, other, w, out, w_out, sems):
    core = at_ref[0] % 2
    copies = [pltpu.make_async_copy(w, w_out, sems.at[0, 4])]
    for i in range(4):
        rows = pl.ds(i * 128, 128)
        copies.append(pltpu.make_async_copy(half.at[rows], out.at[core, rows], sems.at[0, i]))
        copies.append(pltpu.make_async_copy(other.at[rows], out.at[1 - core, rows], sems.at[1, i]))
    for copy in copies:
        copy.start()
    for copy in copies:
        copy.wait()


def per_device(grad_out, relu_mask, saved_agg, weight, tile_vals, tile_pos, tile_count):
    pp = lax.ppermute
    at = jnp.stack([lax.axis_index("row"), lax.axis_index("col"), lax.axis_index("ch")]).astype(jnp.int32)
    (masked,) = call(mask_kernel, "mask", [shape(512, 256)], grad_out, relu_mask, scalars=0)
    left, right = pp(masked, "col", ring4(1)), pp(masked, "col", ring4(-1))
    agg_mate = pp(saved_agg, "ch", AGG_PAIRS)
    masked_mate = pp(masked, "ch", MASK_PAIRS)

    hi, lo = prep(tile_pos.reshape(128), tile_count.reshape(1), tile_vals.reshape(128, 128, 128))
    (part,) = pieces(at, hi, lo, [masked, masked], [(0, 0), (0, 1)])
    la, rb = call(halves_kernel, "halves", [shape(256, 256)] * 2, left, right, part, scalars=0)
    oa, ob = pp(la, "col", ring4(1)), pp(rb, "col", ring4(-1))
    (part,) = pieces(at, hi, lo, [la, left, right, rb], [(3, 0), (3, 1), (1, 0), (1, 1)], base=part)
    w_keep, w_send, token = call(
        wgrad_kernel, "wgrad", [shape(4, 128, 256)] * 2 + [shape(8, 128)], at, saved_agg, agg_mate, masked, masked_mate,
        scratch=[pltpu.VMEM((2, 512, 256), F32)],
    )
    w_recv = pp(w_send, "row", CORE)
    send, keep = pieces(at, hi, lo, [oa, ob], [(2, 0), (2, 1)], base=part, after=token, last=True)

    recv = pp(send, "row", CORE)
    w_own, w_other = call(w_parts_kernel, "w_parts", [shape(4, 64, 256)] * 2, w_keep, w_recv, scalars=0)
    w_mate = pp(w_other, "ch", MASK_PAIRS)
    h_kept, h_send = call(
        h_first_kernel, "h_first", [shape(4, 64, 256)] * 2, at, keep.reshape(8, 64, 256), recv.reshape(8, 64, 256)
    )
    h_pair = pp(h_send, "row", PAIR)
    w_msgs = call(w_spread_kernel, "w_spread", [shape(128, 256)] * 4, at, w_own, w_mate, h_kept)
    t = [w_msgs[0]] + [pp(w_msgs[d], "col", ring4(d)) for d in (1, 2, 3)]
    h_parts = call(h_second_kernel, "h_second", [shape(64, 256)] * 4, t[1], h_kept, h_pair, scalars=0)
    h_got = [pp(h_parts[j], "row", z_shift(2 * j)) for j in (2, 1, 3)]
    (h,) = call(total_kernel, "h_total", [shape(64, 256)], h_parts[0], *h_got, scalars=0)
    hs = [h] + [pp(h, "ch", ring4(d)) for d in (1, 2, 3)]
    own_out, own_w, *msgs = call(
        finish_kernel, "finish", [shape(64, 256), shape(16, 256)] + [shape(80, 256)] * 7, at, *hs, weight, *t
    )
    got = [pp(msg, "row", z_shift(d)) for msg, d in zip(msgs, FAR_FIRST)]
    half, w = call(
        gather_kernel, "gather", [shape(8, 64, 256), shape(16, 256)], at, own_out, own_w, *got
    )
    half = half.reshape(512, 256)
    other = pp(half, "row", CORE)
    input_grad, weight_grad = call(
        last_kernel, "last", [shape(2, 512, 256), shape(16, 256)], at, half, other, w, out_hbm=(0, 1),
        scratch=[pltpu.SemaphoreType.DMA((2, 5))],
    )
    return weight_grad, input_grad.reshape(1024, 256)


def solution(mesh):
    in_specs = (
        P(("row", "col"), "ch"),
        P(("row", "col"), "ch"),
        P(("row", "col"), "ch"),
        P("ch", None),
        P("row", "col", None, None, None),
        P("row", "col", None),
        P("row", "col"),
    )
    out_specs = (P(("row", "col"), "ch"), P("col", "ch"))
    return jax.shard_map(
        per_device, mesh=mesh, in_specs=in_specs, out_specs=out_specs, check_vma=False
    )
```

```python
import functools

import jax
import jax.numpy as jnp
from jax import lax
from jax.experimental import pallas as pl
from jax.experimental.pallas import tpu as pltpu
from jax.sharding import PartitionSpec as P

F32 = jnp.float32
BF16 = jnp.bfloat16
MB = 1 << 20
GROUP = 16
NN = (((1,), (0,)), ((), ()))
TN = (((0,), (0,)), ((), ()))
NT = (((1,), (1,)), ((), ()))

AGG_PAIRS = [(0, 1), (1, 0), (2, 3), (3, 2)]
MASK_PAIRS = [(0, 3), (3, 0), (1, 2), (2, 1)]
CORE = [(r, r ^ 1) for r in range(16)]


PAIR = [(r, ((r // 2 + 1 - 2 * ((r // 2 + r) % 2)) % 8) * 2 + r % 2) for r in range(16)]
FAR_FIRST = (4, 3, 5, 2, 6, 1, 7)


def z_shift(d):
    return [(r, ((r // 2 + d) % 8) * 2 + r % 2) for r in range(16)]


def ring4(d):
    return [(i, (i + d) % 4) for i in range(4)]


def params(mb=32):
    return pltpu.CompilerParams(vmem_limit_bytes=mb * MB)


def shape(*dims, dtype=F32):
    return jax.ShapeDtypeStruct(dims, dtype)


def split(x):
    hi = x.astype(BF16)
    return hi, (x - hi.astype(F32)).astype(BF16)


def dot3(a, b, dims):
    (ah, al), (bh, bl) = a, b

    def one(p, q):
        return lax.dot_general(p, q, dims, preferred_element_type=F32)

    return one(ah, bh) + (one(ah, bl) + one(al, bh))


VMEM = pl.BlockSpec(memory_space=pltpu.VMEM)
SMEM = pl.BlockSpec(memory_space=pltpu.SMEM)
HBM = pl.BlockSpec(memory_space=pltpu.HBM)


def call(kernel, name, out_shape, *args, scalars=1, in_hbm=(), out_hbm=(), scratch=(), mb=12, alias=None):
    ins = [SMEM] * scalars + [HBM if i in in_hbm else VMEM for i in range(len(args) - scalars)]
    outs = [HBM if i in out_hbm else VMEM for i in range(len(out_shape))]
    return pl.pallas_call(
        kernel,
        in_specs=ins,
        out_specs=outs,
        out_shape=out_shape,
        scratch_shapes=list(scratch),
        input_output_aliases=alias or {},
        compiler_params=params(mb),
        name=name,
    )(*args)


def mask_kernel(g_ref, m_ref, full_ref):
    full_ref[...] = g_ref[...] * m_ref[...].astype(F32)


def halves_kernel(left_ref, right_ref, after_ref, a_ref, b_ref):
    a_ref[...] = left_ref[:256, :]
    b_ref[...] = right_ref[256:, :]


def prep_kernel(pos_ref, cnt_ref, tv_hbm, hi_ref, lo_ref, tv_ref, sems):
    cnt = cnt_ref[0]
    chunks = 128 // GROUP
    copies = []
    for g in range(chunks):
        slots = pl.ds(g * GROUP, GROUP)
        copies.append(pltpu.make_async_copy(tv_hbm.at[slots], tv_ref.at[slots], sems.at[g]))
    for copy in copies:
        copy.start()

    def body(s, carry):
        p = pos_ref[s]
        out_tile = p // 8
        hi, lo = split(jnp.where(s < cnt, tv_ref[s], 0.0).T)
        rows = pl.ds(pl.multiple_of((p % 8) * 128, 128), 128)
        cols = pl.ds(pl.multiple_of((out_tile % 2) * 128, 128), 128)
        hi_ref[out_tile // 2, rows, cols] = hi
        lo_ref[out_tile // 2, rows, cols] = lo
        return carry

    for g in range(chunks):
        copies[g].wait()
        lax.fori_loop(g * GROUP, (g + 1) * GROUP, body, 0, unroll=8)


def prep(pos, cnt, tile_vals):
    return call(
        prep_kernel, "prep", [shape(8, 1024, 256, dtype=BF16)] * 2, pos, cnt, tile_vals,
        scalars=2, in_hbm=(0,), mb=40,
        scratch=[pltpu.VMEM((128, 128, 128), F32), pltpu.SemaphoreType.DMA((128 // GROUP,))],
    )


def pieces_kernel(places, has_base, is_last, at_ref, hi_ref, lo_ref, *refs):
    n = len(places)
    core, col = at_ref[0] % 2, at_ref[1]
    ms, rest = refs[:n], refs[n:]
    base = rest[0] if has_base else None
    outs = rest[-2:] if is_last else rest[-1:]
    parts, index = [], []
    for m, (off, part) in zip(ms, places):
        rows = slice(256 * part, 256 * part + 256) if m.shape[0] == 512 else slice(0, 256)
        parts.append(split(m[rows, :]))
        index.append(2 * ((col + off) % 4) + part)
    for i in range(2):
        start = 512 * (i + (1 - 2 * i) * (1 - core)) if is_last else 512 * i
        rows = pl.ds(pl.multiple_of(start, 512), 512)
        acc = None
        for j in range(n):
            term = dot3((hi_ref[index[j], rows, :], lo_ref[index[j], rows, :]), parts[j], NN)
            acc = term if acc is None else acc + term
        if has_base:
            acc = acc + base[rows, :]
        if is_last:
            outs[i][...] = acc
        else:
            outs[0][rows, :] = acc


def pieces(at, hi, lo, ms, places, base=None, after=None, last=False):
    return call(
        functools.partial(pieces_kernel, places, base is not None, last),
        "pieces_last" if last else "pieces",
        [shape(512, 256)] * 2 if last else [shape(1024, 256)],
        at, hi, lo, *ms, *([] if base is None else [base]), *([] if after is None else [after]),
    )


def wgrad_kernel(at_ref, a0, a1, m0, m1, keep, send, token, res):
    core, k = at_ref[0] % 2, at_ref[2]
    token[...] = jnp.zeros_like(token)
    aggs = [split(a0[...]), split(a1[...])]
    grads = [split(m0[...]), split(m1[...])]
    for i in range(2):
        rows = pl.ds(pl.multiple_of(((k + i) % 2) * 256, 256), 256)
        for part in range(2):
            res[part, rows, :] = dot3(aggs[i], grads[part], TN)
    for part in range(2):
        for zz in range(4):
            for c in range(4):
                to = slice((part * 4 + zz) * 16, (part * 4 + zz) * 16 + 16)
                mine = pl.multiple_of(zz * 128 + core * 64 + c * 16, 16)
                other = pl.multiple_of(zz * 128 + (1 - core) * 64 + c * 16, 16)
                keep[c, to, :] = res[part, pl.ds(mine, 16), :]
                send[c, to, :] = res[part, pl.ds(other, 16), :]


def w_spread_kernel(at_ref, keep, recv, *outs):
    c = at_ref[1]
    for d in range(4):
        j = (c + d) % 4
        outs[d][...] = keep[j] + recv[j]


def h_first_kernel(at_ref, keep, recv, kept, send):
    core, z = at_ref[0] % 2, at_ref[0] // 2
    mate = z + 1 - 2 * ((z + core) % 2)
    for j in range(4):
        a, b = (z + 2 * j) % 8, (mate + 8 + 2 * j) % 8
        kept[j] = keep[a] + recv[a]
        send[j] = keep[b] + recv[b]


def h_second_kernel(kept, recv, *outs):
    for j in range(4):
        outs[j][...] = kept[j] + recv[j]


def total_kernel(h0, h1, h2, h3, t0, t1, t2, t3, h, h_and_t, own_t):
    total = (h0[...] + h1[...]) + (h2[...] + h3[...])
    h[...] = total
    h_and_t[:64, :] = total
    t = (t0[...] + t1[...]) + (t2[...] + t3[...])
    own_t[...] = t[:64]
    h_and_t[64:, :] = t[64:]


def finish_kernel(at_ref, h0, h1, h2, h3, w_ref, t, own_out, own_w, *msgs):
    z, k = at_ref[0] // 2, at_ref[2]
    acc = None
    for d, h in enumerate((h0, h1, h2, h3)):
        co = pl.multiple_of(((k + 4 - d) % 4) * 256, 256)
        term = dot3(split(h[:64, :]), split(w_ref[:, pl.ds(co, 256)]), NT)
        acc = term if acc is None else acc + term
    own_out[...] = acc

    def share(j):
        mine = pl.ds(pl.multiple_of((j % 4) * 16, 16), 16)
        mates = pl.ds(pl.multiple_of(64 + (j % 4) * 16, 16), 16)
        theirs = jnp.where(k % 2 == 0, h1[mates, :], h3[mates, :])
        return jnp.where(j // 4 == k // 2, t[mine, :], theirs)

    own_w[...] = share(z)
    for msg, d in zip(msgs, FAR_FIRST):
        msg[:64, :] = acc
        msg[64:, :] = share((z + d) % 8)


def gather_kernel(at_ref, own_out, own_w, *refs):
    z = at_ref[0] // 2
    msgs, half, w = refs[:7], refs[7], refs[8]
    half[z] = own_out[...]
    total = own_w[...]
    for msg, d in zip(msgs, FAR_FIRST):
        half[(z + 8 - d) % 8] = msg[:64, :]
        total += msg[64:, :]
    w[...] = total


def last_kernel(at_ref, half, other, w, out, w_out, sems):
    core = at_ref[0] % 2
    copies = [pltpu.make_async_copy(w, w_out, sems.at[0, 4])]
    for i in range(4):
        rows = pl.ds(i * 128, 128)
        copies.append(pltpu.make_async_copy(half.at[rows], out.at[core, rows], sems.at[0, i]))
        copies.append(pltpu.make_async_copy(other.at[rows], out.at[1 - core, rows], sems.at[1, i]))
    for copy in copies:
        copy.start()
    for copy in copies:
        copy.wait()


def per_device(grad_out, relu_mask, saved_agg, weight, tile_vals, tile_pos, tile_count):
    pp = lax.ppermute
    at = jnp.stack([lax.axis_index("row"), lax.axis_index("col"), lax.axis_index("ch")]).astype(jnp.int32)
    (masked,) = call(mask_kernel, "mask", [shape(512, 256)], grad_out, relu_mask, scalars=0)
    left, right = pp(masked, "col", ring4(1)), pp(masked, "col", ring4(-1))
    agg_mate = pp(saved_agg, "ch", AGG_PAIRS)
    masked_mate = pp(masked, "ch", MASK_PAIRS)

    hi, lo = prep(tile_pos.reshape(128), tile_count.reshape(1), tile_vals.reshape(128, 128, 128))
    (part,) = pieces(at, hi, lo, [masked, masked], [(0, 0), (0, 1)])
    la, rb = call(halves_kernel, "halves", [shape(256, 256)] * 2, left, right, part, scalars=0)
    oa, ob = pp(la, "col", ring4(1)), pp(rb, "col", ring4(-1))
    (part,) = pieces(at, hi, lo, [la, left, right, rb], [(3, 0), (3, 1), (1, 0), (1, 1)], base=part)
    w_keep, w_send, token = call(
        wgrad_kernel, "wgrad", [shape(4, 128, 256)] * 2 + [shape(8, 128)], at, saved_agg, agg_mate, masked, masked_mate,
        scratch=[pltpu.VMEM((2, 512, 256), F32)],
    )
    w_recv = pp(w_send, "row", CORE)
    send, keep = pieces(at, hi, lo, [oa, ob], [(2, 0), (2, 1)], base=part, after=token, last=True)

    recv = pp(send, "row", CORE)
    send, keep = pieces(at, hi, lo, [oa, ob], [(2, 0), (2, 1)], base=part, after=token, last=True)

    recv = pp(send, "row", CORE)
    w_msgs = call(w_spread_kernel, "w_spread", [shape(128, 256)] * 4, at, w_keep, w_recv)
    t = [w_msgs[0]] + [pp(w_msgs[d], "col", ring4(d)) for d in (1, 2, 3)]
    h_kept, h_send = call(
        h_first_kernel, "h_first", [shape(4, 64, 256)] * 2, at, keep.reshape(8, 64, 256), recv.reshape(8, 64, 256)
    )
    h_pair = pp(h_send, "row", PAIR)
    h_parts = call(h_second_kernel, "h_second", [shape(64, 256)] * 4, h_kept, h_pair, scalars=0)
    h_got = [pp(h_parts[j], "row", z_shift(2 * j)) for j in (2, 1, 3)]
    h, h_and_t, own_t = call(
        total_kernel, "h_total", [shape(64, 256), shape(128, 256), shape(64, 256)], h_parts[0], *h_got, *t, scalars=0
    )
    hs = [h] + [pp(p, "ch", ring4(d)) for p, d in ((h_and_t, 1), (h, 2), (h_and_t, 3))]
    own_out, own_w, *msgs = call(
        finish_kernel, "finish", [shape(64, 256), shape(16, 256)] + [shape(80, 256)] * 7, at, *hs, weight, own_t
    )
    got = [pp(msg, "row", z_shift(d)) for msg, d in zip(msgs, FAR_FIRST)]
    half, w = call(
        gather_kernel, "gather", [shape(8, 64, 256), shape(16, 256)], at, own_out, own_w, *got
    )
    half = half.reshape(512, 256)
    other = pp(half, "row", CORE)
    input_grad, weight_grad = call(
        last_kernel, "last", [shape(2, 512, 256), shape(16, 256)], at, half, other, w, out_hbm=(0, 1),
        scratch=[pltpu.SemaphoreType.DMA((2, 5))],
    )
    return weight_grad, input_grad.reshape(1024, 256)


def solution(mesh):
    in_specs = (
        P(("row", "col"), "ch"),
        P(("row", "col"), "ch"),
        P(("row", "col"), "ch"),
        P("ch", None),
        P("row", "col", None, None, None),
        P("row", "col", None),
        P("row", "col"),
    )
    out_specs = (P(("row", "col"), "ch"), P("col", "ch"))
    return jax.shard_map(
        per_device, mesh=mesh, in_specs=in_specs, out_specs=out_specs, check_vma=False
    )
```

```python
import functools

import jax
import jax.numpy as jnp
from jax import lax
from jax.experimental import pallas as pl
from jax.experimental.pallas import tpu as pltpu
from jax.sharding import PartitionSpec as P

F32 = jnp.float32
BF16 = jnp.bfloat16
MB = 1 << 20
GROUP = 16
NN = (((1,), (0,)), ((), ()))
TN = (((0,), (0,)), ((), ()))
NT = (((1,), (1,)), ((), ()))

AGG_PAIRS = [(0, 1), (1, 0), (2, 3), (3, 2)]
MASK_PAIRS = [(0, 3), (3, 0), (1, 2), (2, 1)]
CORE = [(r, r ^ 1) for r in range(16)]


PAIR = [(r, ((r // 2 + 1 - 2 * ((r // 2 + r) % 2)) % 8) * 2 + r % 2) for r in range(16)]
FAR_FIRST = (4, 3, 5, 2, 6, 1, 7)


def z_shift(d):
    return [(r, ((r // 2 + d) % 8) * 2 + r % 2) for r in range(16)]


def ring4(d):
    return [(i, (i + d) % 4) for i in range(4)]


def params(mb=32):
    return pltpu.CompilerParams(vmem_limit_bytes=mb * MB)


def shape(*dims, dtype=F32):
    return jax.ShapeDtypeStruct(dims, dtype)


def split(x):
    hi = x.astype(BF16)
    return hi, (x - hi.astype(F32)).astype(BF16)


def dot3(a, b, dims):
    (ah, al), (bh, bl) = a, b

    def one(p, q):
        return lax.dot_general(p, q, dims, preferred_element_type=F32)

    return one(ah, bh) + (one(ah, bl) + one(al, bh))


VMEM = pl.BlockSpec(memory_space=pltpu.VMEM)
SMEM = pl.BlockSpec(memory_space=pltpu.SMEM)
HBM = pl.BlockSpec(memory_space=pltpu.HBM)


def call(kernel, name, out_shape, *args, scalars=0, in_hbm=(), out_hbm=(), scratch=(), mb=12):
    ins = [SMEM] * scalars + [HBM if i in in_hbm else VMEM for i in range(len(args) - scalars)]
    outs = [HBM if i in out_hbm else VMEM for i in range(len(out_shape))]
    return pl.pallas_call(
        kernel,
        in_specs=ins,
        out_specs=outs,
        out_shape=out_shape,
        scratch_shapes=list(scratch),
        compiler_params=params(mb),
        name=name,
    )(*args)


def mask_kernel(g_ref, m_ref, full_ref):
    full_ref[...] = g_ref[...] * m_ref[...].astype(F32)


def half_kernel(part, whole_ref, after_ref, half_ref):
    half_ref[...] = whole_ref[256 * part : 256 * part + 256, :]


def prep_kernel(pos_ref, cnt_ref, tv_hbm, hi_ref, lo_ref, tv_ref, sems):
    cnt = cnt_ref[0]
    chunks = 128 // GROUP
    copies = []
    for g in range(chunks):
        slots = pl.ds(g * GROUP, GROUP)
        copies.append(pltpu.make_async_copy(tv_hbm.at[slots], tv_ref.at[slots], sems.at[g]))
    for copy in copies:
        copy.start()

    def body(s, carry):
        p = pos_ref[s]
        out_tile = p // 8
        hi, lo = split(jnp.where(s < cnt, tv_ref[s], 0.0).T)
        rows = pl.ds(pl.multiple_of((p % 8) * 128, 128), 128)
        cols = pl.ds(pl.multiple_of((out_tile % 2) * 128, 128), 128)
        hi_ref[out_tile // 2, rows, cols] = hi
        lo_ref[out_tile // 2, rows, cols] = lo
        return carry

    for g in range(chunks):
        copies[g].wait()
        lax.fori_loop(g * GROUP, (g + 1) * GROUP, body, 0, unroll=8)


def prep(pos, cnt, tile_vals):
    return call(
        prep_kernel, "prep", [shape(8, 1024, 256, dtype=BF16)] * 2, pos, cnt, tile_vals,
        scalars=2, in_hbm=(0,), mb=40,
        scratch=[pltpu.VMEM((128, 128, 128), F32), pltpu.SemaphoreType.DMA((128 // GROUP,))],
    )


def pieces_kernel(places, has_base, is_last, hi_ref, lo_ref, *refs):
    n = len(places)
    core, col = lax.axis_index("row") % 2, lax.axis_index("col")
    ms, rest = refs[:n], refs[n:]
    base = rest[0] if has_base else None
    outs = rest[-2:] if is_last else rest[-1:]
    parts, index = [], []
    for m, (off, part) in zip(ms, places):
        rows = slice(256 * part, 256 * part + 256) if m.shape[0] == 512 else slice(0, 256)
        parts.append(split(m[rows, :]))
        index.append(2 * ((col + off) % 4) + part)
    for i in range(2):
        start = 512 * (i + (1 - 2 * i) * (1 - core)) if is_last else 512 * i
        rows = pl.ds(pl.multiple_of(start, 512), 512)
        acc = None
        for j in range(n):
            term = dot3((hi_ref[index[j], rows, :], lo_ref[index[j], rows, :]), parts[j], NN)
            acc = term if acc is None else acc + term
        if has_base:
            acc = acc + base[rows, :]
        if is_last:
            outs[i][...] = acc
        else:
            outs[0][rows, :] = acc


def pieces(hi, lo, ms, places, base=None, after=None, last=False):
    return call(
        functools.partial(pieces_kernel, places, base is not None, last),
        "pieces_last" if last else "pieces",
        [shape(512, 256)] * 2 if last else [shape(1024, 256)],
        hi, lo, *ms, *([] if base is None else [base]), *([] if after is None else [after]),
    )


def wgrad_kernel(a0, a1, m0, m1, keep, send, token, res):
    core, k = lax.axis_index("row") % 2, lax.axis_index("ch")
    token[...] = jnp.zeros_like(token)
    aggs = [split(a0[...]), split(a1[...])]
    grads = [split(m0[...]), split(m1[...])]
    for i in range(2):
        rows = pl.ds(pl.multiple_of(((k + i) % 2) * 256, 256), 256)
        for part in range(2):
            res[part, rows, :] = dot3(aggs[i], grads[part], TN)
    for part in range(2):
        for zz in range(4):
            for c in range(4):
                to = slice((part * 4 + zz) * 16, (part * 4 + zz) * 16 + 16)
                mine = pl.multiple_of(zz * 128 + core * 64 + c * 16, 16)
                other = pl.multiple_of(zz * 128 + (1 - core) * 64 + c * 16, 16)
                keep[c, to, :] = res[part, pl.ds(mine, 16), :]
                send[c, to, :] = res[part, pl.ds(other, 16), :]


def w_spread_kernel(keep, recv, *outs):
    c = lax.axis_index("col")
    for d in range(4):
        j = (c + d) % 4
        outs[d][...] = keep[j] + recv[j]


def h_first_kernel(keep, recv, kept, send):
    core, z = lax.axis_index("row") % 2, lax.axis_index("row") // 2
    mate = z + 1 - 2 * ((z + core) % 2)
    for j in range(4):
        a, b = (z + 2 * j) % 8, (mate + 8 + 2 * j) % 8
        kept[j] = keep[a] + recv[a]
        send[j] = keep[b] + recv[b]


def h_second_kernel(kept, recv, *outs):
    for j in range(4):
        outs[j][...] = kept[j] + recv[j]


def total_kernel(h0, h1, h2, h3, t0, t1, t2, t3, h, h_and_t, own_t):
    total = (h0[...] + h1[...]) + (h2[...] + h3[...])
    h[...] = total
    h_and_t[:64, :] = total
    t = (t0[...] + t1[...]) + (t2[...] + t3[...])
    own_t[...] = t[:64]
    h_and_t[64:, :] = t[64:]


def finish_kernel(h0, h1, h2, h3, w_ref, t, own_out, own_w, *msgs):
    z, k = lax.axis_index("row") // 2, lax.axis_index("ch")
    acc = None
    for d, h in enumerate((h0, h1, h2, h3)):
        co = pl.multiple_of(((k + 4 - d) % 4) * 256, 256)
        term = dot3(split(h[:64, :]), split(w_ref[:, pl.ds(co, 256)]), NT)
        acc = term if acc is None else acc + term
    own_out[...] = acc

    def share(j):
        mine = pl.ds(pl.multiple_of((j % 4) * 16, 16), 16)
        mates = pl.ds(pl.multiple_of(64 + (j % 4) * 16, 16), 16)
        theirs = jnp.where(k % 2 == 0, h1[mates, :], h3[mates, :])
        return jnp.where(j // 4 == k // 2, t[mine, :], theirs)

    own_w[...] = share(z)
    for msg, d in zip(msgs, FAR_FIRST):
        msg[:64, :] = acc
        msg[64:, :] = share((z + d) % 8)


def gather_kernel(own_out, own_w, *refs):
    z = lax.axis_index("row") // 2
    msgs, half, w = refs[:7], refs[7], refs[8]
    half[z] = own_out[...]
    total = own_w[...]
    for msg, d in zip(msgs, FAR_FIRST):
        half[(z + 8 - d) % 8] = msg[:64, :]
        total += msg[64:, :]
    w[...] = total


def last_kernel(half, other, w, out, w_out, sems):
    core = lax.axis_index("row") % 2
    copies = [pltpu.make_async_copy(w, w_out, sems.at[0, 4])]
    for i in range(4):
        rows = pl.ds(i * 128, 128)
        copies.append(pltpu.make_async_copy(half.at[rows], out.at[core, rows], sems.at[0, i]))
        copies.append(pltpu.make_async_copy(other.at[rows], out.at[1 - core, rows], sems.at[1, i]))
    for copy in copies:
        copy.start()
    for copy in copies:
        copy.wait()


def per_device(grad_out, relu_mask, saved_agg, weight, tile_vals, tile_pos, tile_count):
    pp = lax.ppermute
    (masked,) = call(mask_kernel, "mask", [shape(512, 256)], grad_out, relu_mask)
    left, right = pp(masked, "col", ring4(1)), pp(masked, "col", ring4(-1))
    agg_mate = pp(saved_agg, "ch", AGG_PAIRS)
    masked_mate = pp(masked, "ch", MASK_PAIRS)

    hi, lo = prep(tile_pos.reshape(128), tile_count.reshape(1), tile_vals.reshape(128, 128, 128))
    (part,) = pieces(hi, lo, [masked, masked], [(0, 0), (0, 1)])
    (la,) = call(functools.partial(half_kernel, 0), "left_half", [shape(256, 256)], left, part)
    (rb,) = call(functools.partial(half_kernel, 1), "right_half", [shape(256, 256)], right, part)
    oa, ob = pp(la, "col", ring4(1)), pp(rb, "col", ring4(-1))
    (part,) = pieces(hi, lo, [la, left, right, rb], [(3, 0), (3, 1), (1, 0), (1, 1)], base=part)
    w_keep, w_send, token = call(
        wgrad_kernel, "wgrad", [shape(4, 128, 256)] * 2 + [shape(8, 128)], saved_agg, agg_mate, masked, masked_mate,
        scratch=[pltpu.VMEM((2, 512, 256), F32)],
    )
    w_recv = pp(w_send, "row", CORE)
    send, keep = pieces(hi, lo, [oa, ob], [(2, 0), (2, 1)], base=part, after=token, last=True)

    recv = pp(send, "row", CORE)
    w_msgs = call(w_spread_kernel, "w_spread", [shape(128, 256)] * 4, w_keep, w_recv)
    t = [w_msgs[0]] + [pp(w_msgs[d], "col", ring4(d)) for d in (1, 2, 3)]
    h_kept, h_send = call(
        h_first_kernel, "h_first", [shape(4, 64, 256)] * 2, keep.reshape(8, 64, 256), recv.reshape(8, 64, 256)
    )
    h_pair = pp(h_send, "row", PAIR)
    h_parts = call(h_second_kernel, "h_second", [shape(64, 256)] * 4, h_kept, h_pair)
    h_got = [pp(h_parts[j], "row", z_shift(2 * j)) for j in (2, 1, 3)]
    h, h_and_t, own_t = call(
        total_kernel, "h_total", [shape(64, 256), shape(128, 256), shape(64, 256)], h_parts[0], *h_got, *t, scalars=0
    )
    hs = [h] + [pp(p, "ch", ring4(d)) for p, d in ((h_and_t, 1), (h, 2), (h_and_t, 3))]
    own_out, own_w, *msgs = call(
        finish_kernel, "finish", [shape(64, 256), shape(16, 256)] + [shape(80, 256)] * 7, *hs, weight, own_t
    )
    got = [pp(msg, "row", z_shift(d)) for msg, d in zip(msgs, FAR_FIRST)]
    half, w = call(
        gather_kernel, "gather", [shape(8, 64, 256), shape(16, 256)], own_out, own_w, *got
    )
    half = half.reshape(512, 256)
    other = pp(half, "row", CORE)
    input_grad, weight_grad = call(
        last_kernel, "last", [shape(2, 512, 256), shape(16, 256)], half, other, w, out_hbm=(0, 1),
        scratch=[pltpu.SemaphoreType.DMA((2, 5))],
    )
    return weight_grad, input_grad.reshape(1024, 256)


def solution(mesh):
    in_specs = (
        P(("row", "col"), "ch"),
        P(("row", "col"), "ch"),
        P(("row", "col"), "ch"),
        P("ch", None),
        P("row", "col", None, None, None),
        P("row", "col", None),
        P("row", "col"),
    )
    out_specs = (P(("row", "col"), "ch"), P("col", "ch"))
    return jax.shard_map(
        per_device, mesh=mesh, in_specs=in_specs, out_specs=out_specs, check_vma=False
    )
```

```python
import functools

import jax
import jax.numpy as jnp
from jax import lax
from jax.experimental import pallas as pl
from jax.experimental.pallas import tpu as pltpu
from jax.sharding import PartitionSpec as P

F32 = jnp.float32
BF16 = jnp.bfloat16
MB = 1 << 20
GROUP = 16
NN = (((1,), (0,)), ((), ()))
TN = (((0,), (0,)), ((), ()))
NT = (((1,), (1,)), ((), ()))

AGG_PAIRS = [(0, 1), (1, 0), (2, 3), (3, 2)]
MASK_PAIRS = [(0, 3), (3, 0), (1, 2), (2, 1)]
CORE = [(r, r ^ 1) for r in range(16)]


PAIR = [(r, ((r // 2 + 1 - 2 * ((r // 2 + r) % 2)) % 8) * 2 + r % 2) for r in range(16)]
GATHER_ORDER = (3, 5, 2, 6, 1, 7)


def z_shift(d):
    return [(r, ((r // 2 + d) % 8) * 2 + r % 2) for r in range(16)]


def ring4(d):
    return [(i, (i + d) % 4) for i in range(4)]


def params(mb=32):
    return pltpu.CompilerParams(vmem_limit_bytes=mb * MB)


def shape(*dims, dtype=F32):
    return jax.ShapeDtypeStruct(dims, dtype)


def split(x):
    hi = x.astype(BF16)
    return hi, (x - hi.astype(F32)).astype(BF16)


def dot3(a, b, dims):
    (ah, al), (bh, bl) = a, b

    def one(p, q):
        return lax.dot_general(p, q, dims, preferred_element_type=F32)

    return one(ah, bh) + (one(ah, bl) + one(al, bh))


VMEM = pl.BlockSpec(memory_space=pltpu.VMEM)
SMEM = pl.BlockSpec(memory_space=pltpu.SMEM)
HBM = pl.BlockSpec(memory_space=pltpu.HBM)


def call(kernel, name, out_shape, *args, scalars=0, in_hbm=(), out_hbm=(), scratch=(), mb=12):
    ins = [SMEM] * scalars + [HBM if i in in_hbm else VMEM for i in range(len(args) - scalars)]
    outs = [HBM if i in out_hbm else VMEM for i in range(len(out_shape))]
    return pl.pallas_call(
        kernel,
        in_specs=ins,
        out_specs=outs,
        out_shape=out_shape,
        scratch_shapes=list(scratch),
        compiler_params=params(mb),
        name=name,
    )(*args)


def mask_kernel(g_ref, m_ref, full_ref):
    full_ref[...] = g_ref[...] * m_ref[...].astype(F32)


def half_kernel(part, whole_ref, after_ref, half_ref):
    half_ref[...] = whole_ref[256 * part : 256 * part + 256, :]


def prep_kernel(pos_ref, cnt_ref, tv_hbm, hi_ref, lo_ref, tv_ref, sems):
    cnt = cnt_ref[0]
    chunks = 128 // GROUP
    copies = []
    for g in range(chunks):
        slots = pl.ds(g * GROUP, GROUP)
        copies.append(pltpu.make_async_copy(tv_hbm.at[slots], tv_ref.at[slots], sems.at[g]))
    for copy in copies:
        copy.start()

    def body(s, carry):
        p = pos_ref[s]
        out_tile = p // 8
        hi, lo = split(jnp.where(s < cnt, tv_ref[s], 0.0).T)
        rows = pl.ds(pl.multiple_of((p % 8) * 128, 128), 128)
        cols = pl.ds(pl.multiple_of((out_tile % 2) * 128, 128), 128)
        hi_ref[out_tile // 2, rows, cols] = hi
        lo_ref[out_tile // 2, rows, cols] = lo
        return carry

    for g in range(chunks):
        copies[g].wait()
        lax.fori_loop(g * GROUP, (g + 1) * GROUP, body, 0, unroll=8)


def prep(pos, cnt, tile_vals):
    return call(
        prep_kernel, "prep", [shape(8, 1024, 256, dtype=BF16)] * 2, pos, cnt, tile_vals,
        scalars=2, in_hbm=(0,), mb=40,
        scratch=[pltpu.VMEM((128, 128, 128), F32), pltpu.SemaphoreType.DMA((128 // GROUP,))],
    )


def pieces_kernel(places, has_base, is_last, hi_ref, lo_ref, *refs):
    n = len(places)
    core, col = lax.axis_index("row") % 2, lax.axis_index("col")
    ms, rest = refs[:n], refs[n:]
    base = rest[0] if has_base else None
    outs = rest[-2:] if is_last else rest[-1:]
    parts, index = [], []
    for m, (off, part) in zip(ms, places):
        rows = slice(256 * part, 256 * part + 256) if m.shape[0] == 512 else slice(0, 256)
        parts.append(split(m[rows, :]))
        index.append(2 * ((col + off) % 4) + part)
    for i in range(2):
        start = 512 * (i + (1 - 2 * i) * (1 - core)) if is_last else 512 * i
        rows = pl.ds(pl.multiple_of(start, 512), 512)
        acc = None
        for j in range(n):
            term = dot3((hi_ref[index[j], rows, :], lo_ref[index[j], rows, :]), parts[j], NN)
            acc = term if acc is None else acc + term
        if has_base:
            acc = acc + base[rows, :]
        if is_last:
            outs[i][...] = acc
        else:
            outs[0][rows, :] = acc


def pieces(hi, lo, ms, places, base=None, after=None, last=False):
    return call(
        functools.partial(pieces_kernel, places, base is not None, last),
        "pieces_last" if last else "pieces",
        [shape(512, 256)] * 2 if last else [shape(1024, 256)],
        hi, lo, *ms, *([] if base is None else [base]), *([] if after is None else [after]),
    )


def wgrad_kernel(a0, a1, m0, m1, keep, send, token, res):
    core, k = lax.axis_index("row") % 2, lax.axis_index("ch")
    token[...] = jnp.zeros_like(token)
    aggs = [split(a0[...]), split(a1[...])]
    grads = [split(m0[...]), split(m1[...])]
    for i in range(2):
        rows = pl.ds(pl.multiple_of(((k + i) % 2) * 256, 256), 256)
        for part in range(2):
            res[part, rows, :] = dot3(aggs[i], grads[part], TN)
    for part in range(2):
        for zz in range(4):
            for c in range(4):
                to = slice((part * 4 + zz) * 16, (part * 4 + zz) * 16 + 16)
                mine = pl.multiple_of(zz * 128 + core * 64 + c * 16, 16)
                other = pl.multiple_of(zz * 128 + (1 - core) * 64 + c * 16, 16)
                keep[c, to, :] = res[part, pl.ds(mine, 16), :]
                send[c, to, :] = res[part, pl.ds(other, 16), :]


def w_spread_kernel(keep, recv, *outs):
    c = lax.axis_index("col")
    for d in range(4):
        j = (c + d) % 4
        outs[d][...] = keep[j] + recv[j]


def h_first_kernel(keep, recv, kept, send):
    core, z = lax.axis_index("row") % 2, lax.axis_index("row") // 2
    mate = z + 1 - 2 * ((z + core) % 2)
    for j in range(4):
        a, b = (z + 2 * j) % 8, (mate + 8 + 2 * j) % 8
        kept[j] = keep[a] + recv[a]
        send[j] = keep[b] + recv[b]


def h_second_kernel(kept, recv, *outs):
    for j in range(4):
        outs[j][...] = kept[j] + recv[j]


def total_kernel(h0, h1, h2, h3, t0, t1, t2, t3, h, h_and_t, own_t):
    total = (h0[...] + h1[...]) + (h2[...] + h3[...])
    h[...] = total
    h_and_t[:64, :] = total
    t = (t0[...] + t1[...]) + (t2[...] + t3[...])
    own_t[...] = t[:64]
    h_and_t[64:, :] = t[64:]


def finish_kernel(h0, h1, h2, h3, w_ref, t, own_out, own_w, *msgs):
    z, k = lax.axis_index("row") // 2, lax.axis_index("ch")
    acc = None
    for d, h in enumerate((h0, h1, h2, h3)):
        co = pl.multiple_of(((k + 4 - d) % 4) * 256, 256)
        term = dot3(split(h[:64, :]), split(w_ref[:, pl.ds(co, 256)]), NT)
        acc = term if acc is None else acc + term
    own_out[...] = acc

    def share(j):
        mine = pl.ds(pl.multiple_of((j % 4) * 16, 16), 16)
        mates = pl.ds(pl.multiple_of(64 + (j % 4) * 16, 16), 16)
        theirs = jnp.where(k % 2 == 0, h1[mates, :], h3[mates, :])
        return jnp.where(j // 4 == k // 2, t[mine, :], theirs)

    own_w[...] = share(z)
    msgs[0][:16, :] = share((z + 3) % 8)
    msgs[0][16:80, :] = acc
    msgs[0][80:, :] = share((z + 4) % 8)
    for msg, d in zip(msgs[1:], GATHER_ORDER[1:]):
        msg[:64, :] = acc
        msg[64:, :] = share((z + d) % 8)


def relay_kernel(msg, out):
    out[...] = msg[16:, :]


def gather_kernel(own_out, own_w, *refs):
    z = lax.axis_index("row") // 2
    msgs, half, w = refs[:7], refs[7], refs[8]
    half[z] = own_out[...]
    half[(z + 5) % 8] = msgs[0][16:80, :]
    total = own_w[...] + msgs[0][:16, :]
    for msg, d in zip(msgs[1:], GATHER_ORDER[1:] + (4,)):
        half[(z + 8 - d) % 8] = msg[:64, :]
        total += msg[64:, :]
    w[...] = total


def last_kernel(half, other, w, out, w_out, sems):
    core = lax.axis_index("row") % 2
    copies = [pltpu.make_async_copy(w, w_out, sems.at[0, 4])]
    for i in range(4):
        rows = pl.ds(i * 128, 128)
        copies.append(pltpu.make_async_copy(half.at[rows], out.at[core, rows], sems.at[0, i]))
        copies.append(pltpu.make_async_copy(other.at[rows], out.at[1 - core, rows], sems.at[1, i]))
    for copy in copies:
        copy.start()
    for copy in copies:
        copy.wait()


def per_device(grad_out, relu_mask, saved_agg, weight, tile_vals, tile_pos, tile_count):
    pp = lax.ppermute
    (masked,) = call(mask_kernel, "mask", [shape(512, 256)], grad_out, relu_mask)
    left, right = pp(masked, "col", ring4(1)), pp(masked, "col", ring4(-1))
    agg_mate = pp(saved_agg, "ch", AGG_PAIRS)
    masked_mate = pp(masked, "ch", MASK_PAIRS)

    hi, lo = prep(tile_pos.reshape(128), tile_count.reshape(1), tile_vals.reshape(128, 128, 128))
    (part,) = pieces(hi, lo, [masked, masked], [(0, 0), (0, 1)])
    (la,) = call(functools.partial(half_kernel, 0), "left_half", [shape(256, 256)], left, part)
    (rb,) = call(functools.partial(half_kernel, 1), "right_half", [shape(256, 256)], right, part)
    oa, ob = pp(la, "col", ring4(1)), pp(rb, "col", ring4(-1))
    (part,) = pieces(hi, lo, [la, left, right, rb], [(3, 0), (3, 1), (1, 0), (1, 1)], base=part)
    w_keep, w_send, token = call(
        wgrad_kernel, "wgrad", [shape(4, 128, 256)] * 2 + [shape(8, 128)], saved_agg, agg_mate, masked, masked_mate,
        scratch=[pltpu.VMEM((2, 512, 256), F32)],
    )
    w_recv = pp(w_send, "row", CORE)
    send, keep = pieces(hi, lo, [oa, ob], [(2, 0), (2, 1)], base=part, after=token, last=True)

    recv = pp(send, "row", CORE)
    w_msgs = call(w_spread_kernel, "w_spread", [shape(128, 256)] * 4, w_keep, w_recv)
    t = [w_msgs[0]] + [pp(w_msgs[d], "col", ring4(d)) for d in (1, 2, 3)]
    h_kept, h_send = call(
        h_first_kernel, "h_first", [shape(4, 64, 256)] * 2, keep.reshape(8, 64, 256), recv.reshape(8, 64, 256)
    )
    h_pair = pp(h_send, "row", PAIR)
    h_parts = call(h_second_kernel, "h_second", [shape(64, 256)] * 4, h_kept, h_pair)
    h_got = [pp(h_parts[j], "row", z_shift(2 * j)) for j in (2, 1, 3)]
    h, h_and_t, own_t = call(
        total_kernel, "h_total", [shape(64, 256), shape(128, 256), shape(64, 256)], h_parts[0], *h_got, *t, scalars=0
    )
    h2 = pp(h, "ch", ring4(2))
    hs = [h, pp(h_and_t, "ch", ring4(1)), h2, pp(h_and_t, "ch", ring4(3))]
    own_out, own_w, *msgs = call(
        finish_kernel, "finish", [shape(64, 256), shape(16, 256), shape(96, 256)] + [shape(80, 256)] * 5, *hs, weight, own_t
    )
    got = [pp(msg, "row", z_shift(d)) for msg, d in zip(msgs, GATHER_ORDER)]
    (relayed,) = call(relay_kernel, "relay", [shape(80, 256)], got[0])
    got.append(pp(relayed, "row", z_shift(1)))
    half, w = call(
        gather_kernel, "gather", [shape(8, 64, 256), shape(16, 256)], own_out, own_w, *got
    )
    half = half.reshape(512, 256)
    other = pp(half, "row", CORE)
    input_grad, weight_grad = call(
        last_kernel, "last", [shape(2, 512, 256), shape(16, 256)], half, other, w, out_hbm=(0, 1),
        scratch=[pltpu.SemaphoreType.DMA((2, 5))],
    )
    return weight_grad, input_grad.reshape(1024, 256)


def solution(mesh):
    in_specs = (
        P(("row", "col"), "ch"),
        P(("row", "col"), "ch"),
        P(("row", "col"), "ch"),
        P("ch", None),
        P("row", "col", None, None, None),
        P("row", "col", None),
        P("row", "col"),
    )
    out_specs = (P(("row", "col"), "ch"), P("col", "ch"))
    return jax.shard_map(
        per_device, mesh=mesh, in_specs=in_specs, out_specs=out_specs, check_vma=False
    )
```

```python
import functools

import jax
import jax.numpy as jnp
from jax import lax
from jax.experimental import pallas as pl
from jax.experimental.pallas import tpu as pltpu
from jax.sharding import PartitionSpec as P

F32 = jnp.float32
BF16 = jnp.bfloat16
MB = 1 << 20
GROUP = 16
NN = (((1,), (0,)), ((), ()))
TN = (((0,), (0,)), ((), ()))
NT = (((1,), (1,)), ((), ()))

AGG_PAIRS = [(0, 1), (1, 0), (2, 3), (3, 2)]
MASK_PAIRS = [(0, 3), (3, 0), (1, 2), (2, 1)]
CORE = [(r, r ^ 1) for r in range(16)]


PAIR = [(r, ((r // 2 + 1 - 2 * ((r // 2 + r) % 2)) % 8) * 2 + r % 2) for r in range(16)]
GATHER_ORDER = (3, 6, 2, 1, 7)
RELAYED = (4, 5)


def z_shift(d):
    return [(r, ((r // 2 + d) % 8) * 2 + r % 2) for r in range(16)]


def ring4(d):
    return [(i, (i + d) % 4) for i in range(4)]


def params(mb=32):
    return pltpu.CompilerParams(vmem_limit_bytes=mb * MB)


def shape(*dims, dtype=F32):
    return jax.ShapeDtypeStruct(dims, dtype)


def split(x):
    hi = x.astype(BF16)
    return hi, (x - hi.astype(F32)).astype(BF16)


def dot3(a, b, dims):
    (ah, al), (bh, bl) = a, b

    def one(p, q):
        return lax.dot_general(p, q, dims, preferred_element_type=F32)

    return one(ah, bh) + (one(ah, bl) + one(al, bh))


VMEM = pl.BlockSpec(memory_space=pltpu.VMEM)
SMEM = pl.BlockSpec(memory_space=pltpu.SMEM)
HBM = pl.BlockSpec(memory_space=pltpu.HBM)


def call(kernel, name, out_shape, *args, scalars=0, in_hbm=(), out_hbm=(), scratch=(), mb=12):
    ins = [SMEM] * scalars + [HBM if i in in_hbm else VMEM for i in range(len(args) - scalars)]
    outs = [HBM if i in out_hbm else VMEM for i in range(len(out_shape))]
    return pl.pallas_call(
        kernel,
        in_specs=ins,
        out_specs=outs,
        out_shape=out_shape,
        scratch_shapes=list(scratch),
        compiler_params=params(mb),
        name=name,
    )(*args)


def mask_kernel(g_ref, m_ref, full_ref):
    full_ref[...] = g_ref[...] * m_ref[...].astype(F32)


def half_kernel(part, whole_ref, after_ref, half_ref):
    half_ref[...] = whole_ref[256 * part : 256 * part + 256, :]


def prep_kernel(pos_ref, cnt_ref, tv_hbm, hi_ref, lo_ref, tv_ref, sems):
    cnt = cnt_ref[0]
    chunks = 128 // GROUP
    copies = []
    for g in range(chunks):
        slots = pl.ds(g * GROUP, GROUP)
        copies.append(pltpu.make_async_copy(tv_hbm.at[slots], tv_ref.at[slots], sems.at[g]))
    for copy in copies:
        copy.start()

    def body(s, carry):
        p = pos_ref[s]
        out_tile = p // 8
        hi, lo = split(jnp.where(s < cnt, tv_ref[s], 0.0).T)
        rows = pl.ds(pl.multiple_of((p % 8) * 128, 128), 128)
        cols = pl.ds(pl.multiple_of((out_tile % 2) * 128, 128), 128)
        hi_ref[out_tile // 2, rows, cols] = hi
        lo_ref[out_tile // 2, rows, cols] = lo
        return carry

    for g in range(chunks):
        copies[g].wait()
        lax.fori_loop(g * GROUP, (g + 1) * GROUP, body, 0, unroll=8)


def prep(pos, cnt, tile_vals):
    return call(
        prep_kernel, "prep", [shape(8, 1024, 256, dtype=BF16)] * 2, pos, cnt, tile_vals,
        scalars=2, in_hbm=(0,), mb=40,
        scratch=[pltpu.VMEM((128, 128, 128), F32), pltpu.SemaphoreType.DMA((128 // GROUP,))],
    )


def pieces_kernel(places, has_base, is_last, hi_ref, lo_ref, *refs):
    n = len(places)
    core, col = lax.axis_index("row") % 2, lax.axis_index("col")
    ms, rest = refs[:n], refs[n:]
    base = rest[0] if has_base else None
    outs = rest[-2:] if is_last else rest[-1:]
    parts, index = [], []
    for m, (off, part) in zip(ms, places):
        rows = slice(256 * part, 256 * part + 256) if m.shape[0] == 512 else slice(0, 256)
        parts.append(split(m[rows, :]))
        index.append(2 * ((col + off) % 4) + part)
    for i in range(2):
        start = 512 * (i + (1 - 2 * i) * (1 - core)) if is_last else 512 * i
        rows = pl.ds(pl.multiple_of(start, 512), 512)
        acc = None
        for j in range(n):
            term = dot3((hi_ref[index[j], rows, :], lo_ref[index[j], rows, :]), parts[j], NN)
            acc = term if acc is None else acc + term
        if has_base:
            acc = acc + base[rows, :]
        if is_last:
            outs[i][...] = acc
        else:
            outs[0][rows, :] = acc


def pieces(hi, lo, ms, places, base=None, after=None, last=False):
    return call(
        functools.partial(pieces_kernel, places, base is not None, last),
        "pieces_last" if last else "pieces",
        [shape(512, 256)] * 2 if last else [shape(1024, 256)],
        hi, lo, *ms, *([] if base is None else [base]), *([] if after is None else [after]),
    )


def wgrad_kernel(a0, a1, m0, m1, keep, send, token, res):
    core, k = lax.axis_index("row") % 2, lax.axis_index("ch")
    token[...] = jnp.zeros_like(token)
    aggs = [split(a0[...]), split(a1[...])]
    grads = [split(m0[...]), split(m1[...])]
    for i in range(2):
        rows = pl.ds(pl.multiple_of(((k + i) % 2) * 256, 256), 256)
        for part in range(2):
            res[part, rows, :] = dot3(aggs[i], grads[part], TN)
    for part in range(2):
        for zz in range(4):
            for c in range(4):
                to = slice((part * 4 + zz) * 16, (part * 4 + zz) * 16 + 16)
                mine = pl.multiple_of(zz * 128 + core * 64 + c * 16, 16)
                other = pl.multiple_of(zz * 128 + (1 - core) * 64 + c * 16, 16)
                keep[c, to, :] = res[part, pl.ds(mine, 16), :]
                send[c, to, :] = res[part, pl.ds(other, 16), :]


def w_spread_kernel(keep, recv, *outs):
    c = lax.axis_index("col")
    for d in range(4):
        j = (c + d) % 4
        outs[d][...] = keep[j] + recv[j]


def h_first_kernel(keep, recv, kept, send):
    core, z = lax.axis_index("row") % 2, lax.axis_index("row") // 2
    mate = z + 1 - 2 * ((z + core) % 2)
    for j in range(4):
        a, b = (z + 2 * j) % 8, (mate + 8 + 2 * j) % 8
        kept[j] = keep[a] + recv[a]
        send[j] = keep[b] + recv[b]


def h_second_kernel(kept, recv, *outs):
    for j in range(4):
        outs[j][...] = kept[j] + recv[j]


def total_kernel(h0, h1, h2, h3, t0, t1, t2, t3, h, h_and_t, own_t):
    total = (h0[...] + h1[...]) + (h2[...] + h3[...])
    h[...] = total
    h_and_t[:64, :] = total
    t = (t0[...] + t1[...]) + (t2[...] + t3[...])
    own_t[...] = t[:64]
    h_and_t[64:, :] = t[64:]


def finish_kernel(h0, h1, h2, h3, w_ref, t, own_out, own_w, *msgs):
    z, k = lax.axis_index("row") // 2, lax.axis_index("ch")
    acc = None
    for d, h in enumerate((h0, h1, h2, h3)):
        co = pl.multiple_of(((k + 4 - d) % 4) * 256, 256)
        term = dot3(split(h[:64, :]), split(w_ref[:, pl.ds(co, 256)]), NT)
        acc = term if acc is None else acc + term
    own_out[...] = acc

    def share(j):
        mine = pl.ds(pl.multiple_of((j % 4) * 16, 16), 16)
        mates = pl.ds(pl.multiple_of(64 + (j % 4) * 16, 16), 16)
        theirs = jnp.where(k % 2 == 0, h1[mates, :], h3[mates, :])
        return jnp.where(j // 4 == k // 2, t[mine, :], theirs)

    own_w[...] = share(z)
    for msg, d, onward in zip(msgs[:2], GATHER_ORDER[:2], RELAYED):
        msg[:16, :] = share((z + d) % 8)
        msg[16:80, :] = acc
        msg[80:, :] = share((z + onward) % 8)
    for msg, d in zip(msgs[2:], GATHER_ORDER[2:]):
        msg[:64, :] = acc
        msg[64:, :] = share((z + d) % 8)


def relay_kernel(msg, out):
    out[...] = msg[16:, :]


def gather_kernel(own_out, own_w, *refs):
    z = lax.axis_index("row") // 2
    msgs, half, w = refs[:7], refs[7], refs[8]
    half[z] = own_out[...]
    total = own_w[...]
    for msg, d in zip(msgs[:2], GATHER_ORDER[:2]):
        half[(z + 8 - d) % 8] = msg[16:80, :]
        total += msg[:16, :]
    for msg, d in zip(msgs[2:], GATHER_ORDER[2:] + RELAYED):
        half[(z + 8 - d) % 8] = msg[:64, :]
        total += msg[64:, :]
    w[...] = total


def last_kernel(half, other, w, out, w_out, sems):
    core = lax.axis_index("row") % 2
    copies = [pltpu.make_async_copy(w, w_out, sems.at[0, 4])]
    for i in range(4):
        rows = pl.ds(i * 128, 128)
        copies.append(pltpu.make_async_copy(half.at[rows], out.at[core, rows], sems.at[0, i]))
        copies.append(pltpu.make_async_copy(other.at[rows], out.at[1 - core, rows], sems.at[1, i]))
    for copy in copies:
        copy.start()
    for copy in copies:
        copy.wait()


def per_device(grad_out, relu_mask, saved_agg, weight, tile_vals, tile_pos, tile_count):
    pp = lax.ppermute
    (masked,) = call(mask_kernel, "mask", [shape(512, 256)], grad_out, relu_mask)
    left, right = pp(masked, "col", ring4(1)), pp(masked, "col", ring4(-1))
    agg_mate = pp(saved_agg, "ch", AGG_PAIRS)
    masked_mate = pp(masked, "ch", MASK_PAIRS)

    hi, lo = prep(tile_pos.reshape(128), tile_count.reshape(1), tile_vals.reshape(128, 128, 128))
    (part,) = pieces(hi, lo, [masked, masked], [(0, 0), (0, 1)])
    (la,) = call(functools.partial(half_kernel, 0), "left_half", [shape(256, 256)], left, part)
    (rb,) = call(functools.partial(half_kernel, 1), "right_half", [shape(256, 256)], right, part)
    oa, ob = pp(la, "col", ring4(1)), pp(rb, "col", ring4(-1))
    (part,) = pieces(hi, lo, [la, left, right, rb], [(3, 0), (3, 1), (1, 0), (1, 1)], base=part)
    w_keep, w_send, token = call(
        wgrad_kernel, "wgrad", [shape(4, 128, 256)] * 2 + [shape(8, 128)], saved_agg, agg_mate, masked, masked_mate,
        scratch=[pltpu.VMEM((2, 512, 256), F32)],
    )
    w_recv = pp(w_send, "row", CORE)
    send, keep = pieces(hi, lo, [oa, ob], [(2, 0), (2, 1)], base=part, after=token, last=True)

    recv = pp(send, "row", CORE)
    w_msgs = call(w_spread_kernel, "w_spread", [shape(128, 256)] * 4, w_keep, w_recv)
    t = [w_msgs[0]] + [pp(w_msgs[d], "col", ring4(d)) for d in (1, 2, 3)]
    h_kept, h_send = call(
        h_first_kernel, "h_first", [shape(4, 64, 256)] * 2, keep.reshape(8, 64, 256), recv.reshape(8, 64, 256)
    )
    h_pair = pp(h_send, "row", PAIR)
    h_parts = call(h_second_kernel, "h_second", [shape(64, 256)] * 4, h_kept, h_pair)
    h_got = [pp(h_parts[j], "row", z_shift(2 * j)) for j in (2, 1, 3)]
    h, h_and_t, own_t = call(
        total_kernel, "h_total", [shape(64, 256), shape(128, 256), shape(64, 256)], h_parts[0], *h_got, *t, scalars=0
    )
    h2 = pp(h, "ch", ring4(2))
    hs = [h, pp(h_and_t, "ch", ring4(1)), h2, pp(h_and_t, "ch", ring4(3))]
    own_out, own_w, *msgs = call(
        finish_kernel, "finish", [shape(64, 256), shape(16, 256)] + [shape(96, 256)] * 2 + [shape(80, 256)] * 3, *hs, weight, own_t
    )
    got = [pp(msg, "row", z_shift(d)) for msg, d in zip(msgs, GATHER_ORDER)]
    for msg, d, onward in zip(got[:2], GATHER_ORDER[:2], RELAYED):
        (relayed,) = call(relay_kernel, "relay", [shape(80, 256)], msg)
        got.append(pp(relayed, "row", z_shift(onward - d)))
    half, w = call(
        gather_kernel, "gather", [shape(8, 64, 256), shape(16, 256)], own_out, own_w, *got
    )
    half = half.reshape(512, 256)
    other = pp(half, "row", CORE)
    input_grad, weight_grad = call(
        last_kernel, "last", [shape(2, 512, 256), shape(16, 256)], half, other, w, out_hbm=(0, 1),
        scratch=[pltpu.SemaphoreType.DMA((2, 5))],
    )
    return weight_grad, input_grad.reshape(1024, 256)


def solution(mesh):
    in_specs = (
        P(("row", "col"), "ch"),
        P(("row", "col"), "ch"),
        P(("row", "col"), "ch"),
        P("ch", None),
        P("row", "col", None, None, None),
        P("row", "col", None),
        P("row", "col"),
    )
    out_specs = (P(("row", "col"), "ch"), P("col", "ch"))
    return jax.shard_map(
        per_device, mesh=mesh, in_specs=in_specs, out_specs=out_specs, check_vma=False
    )
```

```python
import functools

import jax
import jax.numpy as jnp
from jax import lax
from jax.experimental import pallas as pl
from jax.experimental.pallas import tpu as pltpu
from jax.sharding import PartitionSpec as P

F32 = jnp.float32
BF16 = jnp.bfloat16
MB = 1 << 20
GROUP = 16
NN = (((1,), (0,)), ((), ()))
TN = (((0,), (0,)), ((), ()))
NT = (((1,), (1,)), ((), ()))

AGG_PAIRS = [(0, 1), (1, 0), (2, 3), (3, 2)]
MASK_PAIRS = [(0, 3), (3, 0), (1, 2), (2, 1)]
CORE = [(r, r ^ 1) for r in range(16)]


PAIR = [(r, ((r // 2 + 1 - 2 * ((r // 2 + r) % 2)) % 8) * 2 + r % 2) for r in range(16)]
GATHER_ORDER = (3, 6, 2, 1, 7)
RELAYED = (4, 5)


def z_shift(d):
    return [(r, ((r // 2 + d) % 8) * 2 + r % 2) for r in range(16)]


def ring4(d):
    return [(i, (i + d) % 4) for i in range(4)]


def params(mb=32):
    return pltpu.CompilerParams(vmem_limit_bytes=mb * MB)


def shape(*dims, dtype=F32):
    return jax.ShapeDtypeStruct(dims, dtype)


def split(x):
    hi = x.astype(BF16)
    return hi, (x - hi.astype(F32)).astype(BF16)


def dot3(a, b, dims):
    (ah, al), (bh, bl) = a, b

    def one(p, q):
        return lax.dot_general(p, q, dims, preferred_element_type=F32)

    return one(ah, bh) + (one(ah, bl) + one(al, bh))


VMEM = pl.BlockSpec(memory_space=pltpu.VMEM)
SMEM = pl.BlockSpec(memory_space=pltpu.SMEM)
HBM = pl.BlockSpec(memory_space=pltpu.HBM)


def call(kernel, name, out_shape, *args, scalars=0, in_hbm=(), out_hbm=(), scratch=(), mb=12):
    ins = [SMEM] * scalars + [HBM if i in in_hbm else VMEM for i in range(len(args) - scalars)]
    outs = [HBM if i in out_hbm else VMEM for i in range(len(out_shape))]
    return pl.pallas_call(
        kernel,
        in_specs=ins,
        out_specs=outs,
        out_shape=out_shape,
        scratch_shapes=list(scratch),
        compiler_params=params(mb),
        name=name,
    )(*args)


def mask_kernel(g_ref, m_ref, full_ref):
    full_ref[...] = g_ref[...] * m_ref[...].astype(F32)


def half_kernel(part, whole_ref, after_ref, half_ref):
    half_ref[...] = whole_ref[256 * part : 256 * part + 256, :]


def prep_kernel(pos_ref, cnt_ref, tv_hbm, hi_ref, lo_ref, tv_ref, sems):
    cnt = cnt_ref[0]
    chunks = 128 // GROUP
    copies = []
    for g in range(chunks):
        slots = pl.ds(g * GROUP, GROUP)
        copies.append(pltpu.make_async_copy(tv_hbm.at[slots], tv_ref.at[slots], sems.at[g]))
    for copy in copies:
        copy.start()

    def body(s, carry):
        p = pos_ref[s]
        out_tile = p // 8
        hi, lo = split(jnp.where(s < cnt, tv_ref[s], 0.0).T)
        rows = pl.ds(pl.multiple_of((p % 8) * 128, 128), 128)
        cols = pl.ds(pl.multiple_of((out_tile % 2) * 128, 128), 128)
        hi_ref[out_tile // 2, rows, cols] = hi
        lo_ref[out_tile // 2, rows, cols] = lo
        return carry

    for g in range(chunks):
        copies[g].wait()
        lax.fori_loop(g * GROUP, (g + 1) * GROUP, body, 0, unroll=8)


def prep(pos, cnt, tile_vals):
    return call(
        prep_kernel, "prep", [shape(8, 1024, 256, dtype=BF16)] * 2, pos, cnt, tile_vals,
        scalars=2, in_hbm=(0,), mb=40,
        scratch=[pltpu.VMEM((128, 128, 128), F32), pltpu.SemaphoreType.DMA((128 // GROUP,))],
    )


def pieces_kernel(places, has_base, is_last, hi_ref, lo_ref, *refs):
    n = len(places)
    core, col = lax.axis_index("row") % 2, lax.axis_index("col")
    ms, rest = refs[:n], refs[n:]
    base = rest[0] if has_base else None
    outs = rest[-2:] if is_last else rest[-1:]
    parts, index = [], []
    for m, (off, part) in zip(ms, places):
        rows = slice(256 * part, 256 * part + 256) if m.shape[0] == 512 else slice(0, 256)
        parts.append(split(m[rows, :]))
        index.append(2 * ((col + off) % 4) + part)
    for i in range(2):
        start = 512 * (i + (1 - 2 * i) * (1 - core)) if is_last else 512 * i
        rows = pl.ds(pl.multiple_of(start, 512), 512)
        acc = None
        for j in range(n):
            term = dot3((hi_ref[index[j], rows, :], lo_ref[index[j], rows, :]), parts[j], NN)
            acc = term if acc is None else acc + term
        if has_base:
            acc = acc + base[rows, :]
        if is_last:
            outs[i][...] = acc
        else:
            outs[0][rows, :] = acc


def pieces(hi, lo, ms, places, base=None, after=None, last=False):
    return call(
        functools.partial(pieces_kernel, places, base is not None, last),
        "pieces_last" if last else "pieces",
        [shape(512, 256)] * 2 if last else [shape(1024, 256)],
        hi, lo, *ms, *([] if base is None else [base]), *([] if after is None else [after]),
    )


def wgrad_kernel(a0, a1, m0, m1, keep, send, token, res):
    core, k = lax.axis_index("row") % 2, lax.axis_index("ch")
    token[...] = jnp.zeros_like(token)
    aggs = [split(a0[...]), split(a1[...])]
    grads = [split(m0[...]), split(m1[...])]
    for i in range(2):
        rows = pl.ds(pl.multiple_of(((k + i) % 2) * 256, 256), 256)
        for part in range(2):
            res[part, rows, :] = dot3(aggs[i], grads[part], TN)
    for part in range(2):
        for zz in range(4):
            for c in range(4):
                to = slice((part * 4 + zz) * 16, (part * 4 + zz) * 16 + 16)
                mine = pl.multiple_of(zz * 128 + core * 64 + c * 16, 16)
                other = pl.multiple_of(zz * 128 + (1 - core) * 64 + c * 16, 16)
                keep[c, to, :] = res[part, pl.ds(mine, 16), :]
                send[c, to, :] = res[part, pl.ds(other, 16), :]


def w_spread_kernel(keep, recv, *outs):
    c = lax.axis_index("col")
    for d in range(4):
        j = (c + d) % 4
        outs[d][...] = keep[j] + recv[j]


def h_first_kernel(keep, recv, kept, send):
    core, z = lax.axis_index("row") % 2, lax.axis_index("row") // 2
    mate = z + 1 - 2 * ((z + core) % 2)
    for j in range(4):
        a, b = (z + 2 * j) % 8, (mate + 8 + 2 * j) % 8
        kept[j] = keep[a] + recv[a]
        send[j] = keep[b] + recv[b]


def h_second_kernel(kept, recv, *outs):
    for j in range(4):
        outs[j][...] = kept[j] + recv[j]


def total_kernel(h0, h1, h2, h3, t0, t1, t2, t3, h, h_and_t, own_t):
    total = (h0[...] + h1[...]) + (h2[...] + h3[...])
    h[...] = total
    h_and_t[:64, :] = total
    t = (t0[...] + t1[...]) + (t2[...] + t3[...])
    own_t[...] = t[:64]
    h_and_t[64:, :] = t[64:]


def finish_kernel(h0, h1, h2, h3, w_ref, t, own_out, own_w, *msgs):
    z, k = lax.axis_index("row") // 2, lax.axis_index("ch")
    acc = None
    for d, h in enumerate((h0, h1, h2, h3)):
        co = pl.multiple_of(((k + 4 - d) % 4) * 256, 256)
        term = dot3(split(h[:64, :]), split(w_ref[:, pl.ds(co, 256)]), NT)
        acc = term if acc is None else acc + term
    own_out[...] = acc

    def share(j):
        mine = pl.ds(pl.multiple_of((j % 4) * 16, 16), 16)
        mates = pl.ds(pl.multiple_of(64 + (j % 4) * 16, 16), 16)
        theirs = jnp.where(k % 2 == 0, h1[mates, :], h3[mates, :])
        return jnp.where(j // 4 == k // 2, t[mine, :], theirs)

    own_w[...] = share(z)
    for msg, d, onward in zip(msgs[:2], GATHER_ORDER[:2], RELAYED):
        msg[:16, :] = share((z + d) % 8)
        msg[16:80, :] = acc
        msg[80:, :] = share((z + onward) % 8)
    for msg, d in zip(msgs[2:], GATHER_ORDER[2:]):
        msg[:64, :] = acc
        msg[64:, :] = share((z + d) % 8)


def relay_kernel(msg, out):
    out[...] = msg[16:, :]


def gather_kernel(own_out, own_w, *refs):
    z = lax.axis_index("row") // 2
    msgs, half, w = refs[:7], refs[7], refs[8]
    half[z] = own_out[...]
    total = own_w[...]
    for msg, d in zip(msgs[:2], GATHER_ORDER[:2]):
        half[(z + 8 - d) % 8] = msg[16:80, :]
        total += msg[:16, :]
    for msg, d in zip(msgs[2:], GATHER_ORDER[2:] + RELAYED):
        half[(z + 8 - d) % 8] = msg[:64, :]
        total += msg[64:, :]
    w[...] = total


def last_kernel(half, other, w, out, w_out, sems):
    core = lax.axis_index("row") % 2
    copies = [pltpu.make_async_copy(w, w_out, sems.at[0, 4])]
    for i in range(4):
        rows = pl.ds(i * 128, 128)
        copies.append(pltpu.make_async_copy(half.at[rows], out.at[core, rows], sems.at[0, i]))
        copies.append(pltpu.make_async_copy(other.at[rows], out.at[1 - core, rows], sems.at[1, i]))
    for copy in copies:
        copy.start()
    for copy in copies:
        copy.wait()


def per_device(grad_out, relu_mask, saved_agg, weight, tile_vals, tile_pos, tile_count):
    pp = lax.ppermute
    (masked,) = call(mask_kernel, "mask", [shape(512, 256)], grad_out, relu_mask)
    left, right = pp(masked, "col", ring4(1)), pp(masked, "col", ring4(-1))
    agg_mate = pp(saved_agg, "ch", AGG_PAIRS)
    masked_mate = pp(masked, "ch", MASK_PAIRS)

    hi, lo = prep(tile_pos.reshape(128), tile_count.reshape(1), tile_vals.reshape(128, 128, 128))
    (part,) = pieces(hi, lo, [masked, masked], [(0, 0), (0, 1)])
    (la,) = call(functools.partial(half_kernel, 0), "left_half", [shape(256, 256)], left, part)
    (rb,) = call(functools.partial(half_kernel, 1), "right_half", [shape(256, 256)], right, part)
    oa, ob = pp(la, "col", ring4(1)), pp(rb, "col", ring4(-1))
    (part,) = pieces(hi, lo, [la, left, right, rb], [(3, 0), (3, 1), (1, 0), (1, 1)], base=part)
    w_keep, w_send, token = call(
        wgrad_kernel, "wgrad", [shape(4, 128, 256)] * 2 + [shape(8, 128)], saved_agg, agg_mate, masked, masked_mate,
        scratch=[pltpu.VMEM((2, 512, 256), F32)],
    )
    w_recv = pp(w_send, "row", CORE)
    send, keep = pieces(hi, lo, [oa, ob], [(2, 0), (2, 1)], base=part, after=token, last=True)

    recv = pp(send, "row", CORE)
    w_msgs = call(w_spread_kernel, "w_spread", [shape(128, 256)] * 4, w_keep, w_recv)
    t = [w_msgs[0]] + [pp(w_msgs[d], "col", ring4(d)) for d in (1, 2, 3)]
    h_kept, h_send = call(
        h_first_kernel, "h_first", [shape(4, 64, 256)] * 2, keep.reshape(8, 64, 256), recv.reshape(8, 64, 256)
    )
    h_pair = pp(h_send, "row", PAIR)
    h_parts = call(h_second_kernel, "h_second", [shape(64, 256)] * 4, h_kept, h_pair)
    h_got = [pp(h_parts[j], "row", z_shift(2 * j)) for j in (1, 3, 2)]
    h, h_and_t, own_t = call(
        total_kernel, "h_total", [shape(64, 256), shape(128, 256), shape(64, 256)], h_parts[0], *h_got, *t, scalars=0
    )
    h2 = pp(h, "ch", ring4(2))
    hs = [h, pp(h_and_t, "ch", ring4(1)), h2, pp(h_and_t, "ch", ring4(3))]
    own_out, own_w, *msgs = call(
        finish_kernel, "finish", [shape(64, 256), shape(16, 256)] + [shape(96, 256)] * 2 + [shape(80, 256)] * 3, *hs, weight, own_t
    )
    got = [pp(msg, "row", z_shift(d)) for msg, d in zip(msgs, GATHER_ORDER)]
    for msg, d, onward in zip(got[:2], GATHER_ORDER[:2], RELAYED):
        (relayed,) = call(relay_kernel, "relay", [shape(80, 256)], msg)
        got.append(pp(relayed, "row", z_shift(onward - d)))
    half, w = call(
        gather_kernel, "gather", [shape(8, 64, 256), shape(16, 256)], own_out, own_w, *got
    )
    half = half.reshape(512, 256)
    other = pp(half, "row", CORE)
    input_grad, weight_grad = call(
        last_kernel, "last", [shape(2, 512, 256), shape(16, 256)], half, other, w, out_hbm=(0, 1),
        scratch=[pltpu.SemaphoreType.DMA((2, 5))],
    )
    return weight_grad, input_grad.reshape(1024, 256)


def solution(mesh):
    in_specs = (
        P(("row", "col"), "ch"),
        P(("row", "col"), "ch"),
        P(("row", "col"), "ch"),
        P("ch", None),
        P("row", "col", None, None, None),
        P("row", "col", None),
        P("row", "col"),
    )
    out_specs = (P(("row", "col"), "ch"), P("col", "ch"))
    return jax.shard_map(
        per_device, mesh=mesh, in_specs=in_specs, out_specs=out_specs, check_vma=False
    )
```
